512 devices in a mesh: tm: 64 (over x, z, y_hi), tmpl: 8 (over y_lo, core).
Axes of the slice: x: 4, y: 8 (y_hi: 2, y_lo: 4; y = y_hi * 4 + y_lo), z: 8, core: 2. Of those that a mesh axis runs over, the one named last changes fastest.
Arguments:
- raw: bfloat16 [2048, 64, 8, 256], P('tm', None, 'tmpl')
- avail: int32 [64, 8, 2048], P(None, 'tmpl', 'tm'), may hold values from 0 to 1, as said below
- templates: bfloat16 [128, 8, 192], P('tmpl'), may hold values from -0.4375 to 0.4375
- stations: int32 [128, 8], replicated, may hold values from 0 to 2047, as said below
- shifts: int32 [128, 8], replicated, may hold values from 0 to 63
Outputs:
- stack: float32 [128, 131072], P(None, ('tm', 'tmpl'))
The draws below stay inside these ranges and needn't reach their ends.
Inputs may be any that keep to these rules, and one draw needn't show every extreme that they name: `avail`: in each window and each block of 32 consecutive station numbers, at least 8 and at most 24 stations are available; every such block has exactly 24 available in some window, and some window has exactly 24 in every block. Each row names 8 different stations.
All inputs are finite; a program needn't handle non-finite values.
Results may differ from the reference program's by a relative error of at most 0.024.
Values may be sent and summed in bfloat16 or wider, within the bound.
No kernel may reach another device: no remote copies, remote signals or barrier semaphores. Data moves between devices by JAX's collectives and lax.ppermute only.
A program may use at most 64 MiB of HBM per device.

```python
import math
import jax
import jax.numpy as jnp
from jax import lax

STATIONS = 2048
W = 256
L = 192
SMAX = 64
K = 8
TEMPLATES = 128
STRETCH = 32
CAP = 24
BLOCKS = 512
N_TMPL = 8


def draw_raw(key, part):
    key = jax.random.fold_in(key, 11)
    keys = jax.random.split(key, 3)
    station_scale = jnp.exp(jax.random.uniform(keys[0], (STATIONS, 1, 1), minval=0.0, maxval=math.log(10.0)))
    block_scale = jnp.exp(jax.random.uniform(keys[1], (1, BLOCKS, 1), minval=0.0, maxval=math.log(10.0)))
    values = jax.random.normal(keys[2], (STATIONS, BLOCKS, W))
    values = values * station_scale * block_scale
    return values.reshape(STATIONS, BLOCKS // N_TMPL, N_TMPL, W).astype(jnp.bfloat16)


def draw_avail(key, part):
    key = jax.random.fold_in(key, 31)
    keys = jax.random.split(key, 4)
    groups = STATIONS // STRETCH
    counts = jax.random.randint(keys[0], (BLOCKS, groups), STRETCH // 4, CAP + 1)
    full_block = jax.random.randint(keys[1], (), 0, BLOCKS)
    per_group = jax.random.randint(keys[2], (groups,), 0, BLOCKS)
    rows = jnp.arange(BLOCKS, dtype=jnp.int32)[:, None]
    counts = jnp.where((rows == full_block) | (rows == per_group[None, :]), CAP, counts)
    scores = jax.random.randint(keys[3], (BLOCKS, groups, STRETCH), 0, 65536) * STRETCH + jnp.arange(STRETCH, dtype=jnp.int32)
    rank = jnp.argsort(jnp.argsort(scores, axis=2), axis=2)
    live = (rank < counts[:, :, None]).astype(jnp.int32)
    return live.reshape(BLOCKS // N_TMPL, N_TMPL, STATIONS)


def draw_stations(key, part):
    key = jax.random.fold_in(key, 23)
    scores = jax.random.randint(key, (TEMPLATES, STATIONS), 0, 65536) * STATIONS + jnp.arange(STATIONS, dtype=jnp.int32)
    order = jnp.argsort(scores, axis=1)
    return order[:, :K].astype(jnp.int32)


def place_ends(drawn, key, least, high):
    dims = drawn.shape
    spot = [jax.random.randint(jax.random.fold_in(key, axis), (), 0, dims[axis]) for axis in range(len(dims))]
    drawn = drawn.at[tuple(spot)].set(least)
    longest = dims.index(max(dims))
    spot[longest] = (spot[longest] + 1) % dims[longest]
    return drawn.at[tuple(spot)].set(high)


def block_levels(key, dims, shards, smallest, top_value):
    factor_of, own = 1.0, jax.random.fold_in(key, 6)
    for dim, parts in shards:
        steps = jnp.exp(jax.random.uniform(jax.random.fold_in(own, dim), (parts,), jnp.float32, smallest / len(shards), top_value / len(shards)))
        factor_of = factor_of * jnp.repeat(steps, dims[dim] // parts).reshape([-1 if axis == dim else 1 for axis in range(len(dims))])
    return factor_of


def noise(rng, extent, spread, limit, pieces=(), kind=jnp.bfloat16):
    gain = block_levels(rng, extent, pieces, -0.22, 0.18) if pieces else 1.0
    drawn = jax.random.normal(rng, extent, jnp.float32) * spread * gain
    return jnp.minimum(jnp.maximum(drawn, -limit), limit).astype(kind)


def setup_inputs(seed: int = 0) -> dict:
    arg_keys = jax.random.split(jax.random.key(seed), 6)
    return {
        "raw": draw_raw(jax.random.fold_in(arg_keys[5], 71), 0),
        "avail": draw_avail(jax.random.fold_in(arg_keys[5], 71), 0),
        "templates": noise(arg_keys[2], (TEMPLATES, K, L), L ** -0.5, 0.4375, ((0, 8),)),
        "stations": draw_stations(jax.random.fold_in(arg_keys[5], 71), 0),
        "shifts": place_ends(jax.random.randint(arg_keys[4], (TEMPLATES, K), 0, SMAX), jax.random.fold_in(arg_keys[4], 1), 0, SMAX - 1).astype(jnp.int32),
    }


epsilon = 1e-05

def reference(raw, avail, templates, stations, shifts):
    span = W + L + SMAX
    signal = raw.reshape(STATIONS, BLOCKS, W)
    status = jnp.transpose(avail.reshape(BLOCKS, STATIONS))
    masked = signal * status.astype(jnp.bfloat16)[:, :, None]
    following = jnp.concatenate([masked[:, 1:, :], jnp.zeros((STATIONS, 1, W), jnp.bfloat16)], axis=1)
    present_all = status.astype(jnp.float32)
    traces = templates.reshape(TEMPLATES * K, L).astype(jnp.float32)
    template_spec = jnp.fft.fft(traces, n=span, axis=1)
    wave_real = lax.optimization_barrier(jnp.real(template_spec).astype(jnp.bfloat16))
    wave_imag = lax.optimization_barrier(jnp.imag(template_spec).astype(jnp.bfloat16))
    wave_real = wave_real.astype(jnp.float32).reshape(TEMPLATES, K, span)
    wave_imag = wave_imag.astype(jnp.float32).reshape(TEMPLATES, K, span)
    frequency = jnp.arange(span, dtype=jnp.int32)
    angle = (shifts[:, :, None] * frequency[None, None, :] % span).astype(jnp.float32) * (2.0 * math.pi / span)
    cosine = jnp.cos(angle)
    sine_part = jnp.sin(angle)

    def one_block(index):
        own = lax.dynamic_index_in_dim(masked, index, 1, keepdims=False)
        after = lax.dynamic_index_in_dim(following, index, 1, keepdims=False)
        present = lax.dynamic_index_in_dim(present_all, index, 1, keepdims=False)
        segment = jnp.concatenate([own, after[:, :span - W]], axis=1).astype(jnp.float32)
        power = lax.optimization_barrier(jnp.mean(jnp.square(own.astype(jnp.float32)), axis=1))
        scaled = (segment * (present * lax.rsqrt(power + epsilon))[:, None]).astype(jnp.bfloat16)
        spectrum = jnp.fft.fft(scaled.astype(jnp.float32), axis=1)
        data_real = lax.optimization_barrier(jnp.real(spectrum).astype(jnp.bfloat16))
        data_imag = lax.optimization_barrier(jnp.imag(spectrum).astype(jnp.bfloat16))
        picked_real = data_real[stations].astype(jnp.float32)
        picked_imag = data_imag[stations].astype(jnp.float32)
        weight = present[stations]
        prod_real = picked_real * wave_real + picked_imag * wave_imag
        prod_imag = picked_imag * wave_real - picked_real * wave_imag
        summed_real = lax.optimization_barrier(jnp.sum(weight[:, :, None] * (prod_real * cosine - prod_imag * sine_part), axis=1))
        summed_imag = lax.optimization_barrier(jnp.sum(weight[:, :, None] * (prod_real * sine_part + prod_imag * cosine), axis=1))
        summed_real = lax.optimization_barrier(summed_real.astype(jnp.bfloat16)).astype(jnp.float32)
        summed_imag = lax.optimization_barrier(summed_imag.astype(jnp.bfloat16)).astype(jnp.float32)
        series = jnp.real(jnp.fft.ifft(lax.complex(summed_real, summed_imag), axis=1))[:, :W]
        number = jnp.maximum(lax.optimization_barrier(jnp.sum(weight, axis=1)), 1.0)
        return (series / number[:, None]).astype(jnp.float32)
    stacks = lax.map(one_block, jnp.arange(BLOCKS, dtype=jnp.int32))
    return jnp.transpose(stacks, (1, 0, 2)).reshape(TEMPLATES, BLOCKS * W)
```

```python
import functools
import math

import jax
import jax.numpy as jnp
import numpy as np
from jax import lax
from jax.experimental import pallas as pl
from jax.experimental.pallas import tpu as pltpu
from jax.sharding import PartitionSpec as P

L = 192
SMAX = 64
CAP = 24
GROUP = 16
MISSING = 4096.0
LIMIT = 3e38

epsilon = 1e-05


def cosine_rows(span, width):
    half = span // 2
    frequency = np.arange(half)[:, None]
    sample = np.arange(width)[None, :]
    angle = (frequency * sample % span) * (2.0 * math.pi / span)
    real = np.cos(angle)
    imag = -np.sin(angle)
    imag[0] = np.cos(math.pi * np.arange(width))
    return real, imag


def forward_rows(span, width):
    real, imag = cosine_rows(span, width)
    return jnp.asarray(np.concatenate([real, imag]).astype(jnp.bfloat16))


def inverse_rows(span, width):
    real, imag = cosine_rows(span, width)
    real, imag = 2.0 * real, 2.0 * imag
    real[0] *= 0.5
    imag[0] *= 0.5
    table = np.concatenate([real, imag])
    flip = np.where(np.arange(span // 2) % 2 == 0, 1.0, -1.0)
    after = table * np.concatenate([flip, flip])[:, None]
    return (
        jnp.asarray(table.T.astype(jnp.bfloat16)),
        jnp.asarray(after.T.astype(jnp.bfloat16)),
    )


def phase_tables(span, moves):
    angle = (np.arange(span // 2)[:, None] * np.arange(moves)[None, :] % span) * (2.0 * math.pi / span)
    parts = []
    for value in (np.cos(angle), np.sin(angle)):
        high = value.astype(jnp.bfloat16)
        parts.append(high)
        parts.append((value - high.astype(np.float64)).astype(jnp.bfloat16))
    return jnp.asarray(np.concatenate(parts))


def dot(a, b):
    return jnp.dot(a, b, preferred_element_type=jnp.float32)


def dot_rows(a, b):
    return lax.dot_general(a, b, (((1,), (1,)), ((), ())), preferred_element_type=jnp.float32)


def iota(shape, dim):
    return lax.broadcasted_iota(jnp.int32, shape, dim)


def to_row(column, eye):
    return jnp.sum(jnp.where(eye, column, 0.0), axis=0, keepdims=True)


def to_column(row, eye):
    return jnp.sum(jnp.where(eye, row, 0.0), axis=1, keepdims=True)


def pack_kernel(avail_ref, raw_ref, out_ref):
    count = raw_ref.shape[0]
    part = raw_ref.shape[1]
    windows = avail_ref.shape[1]
    status = avail_ref[...].astype(jnp.float32)
    flags = jnp.transpose(status).astype(jnp.bfloat16)
    place = (iota((count, 128), 0) == iota((count, 128), 1)).astype(jnp.bfloat16)
    before = (iota((count, 128), 0) < iota((count, 128), 1)).astype(jnp.bfloat16)
    first = pl.program_id(0) * part
    pick = (iota((part, windows), 1) == iota((part, windows), 0) + first).astype(jnp.bfloat16)
    flags = dot(pick, flags).astype(jnp.bfloat16)
    present = dot(flags, place)
    code = jnp.where(present > 0.5, dot(flags, before), MISSING)
    lanes = count * GROUP
    spread = (iota((128, lanes), 0) == iota((128, lanes), 1) // GROUP).astype(jnp.bfloat16)
    for block in range(part // GROUP):
        own = code[block * GROUP : (block + 1) * GROUP]
        wide = dot(own.astype(jnp.bfloat16), spread)
        wide = jnp.where(iota((GROUP, lanes), 1) % GROUP == iota((GROUP, lanes), 0), wide, -1.0)
        slot = iota((GROUP, CAP, lanes), 1).astype(jnp.float32)
        mover = jnp.where(wide[:, None, :] == slot, 1.0, 0.0).reshape(GROUP * CAP, lanes).astype(jnp.bfloat16)
        waves = raw_ref[:, block * GROUP : (block + 1) * GROUP, :].reshape(lanes, raw_ref.shape[2])
        moved = dot(mover, waves)
        for window in range(GROUP):
            rows = moved[window * CAP : (window + 1) * CAP]
            extra = jnp.broadcast_to(own[window : window + 1], (8, 128))
            out_ref[block * GROUP + window] = jnp.concatenate([rows[:, :128], rows[:, 128:], extra], axis=0).astype(
                jnp.bfloat16
            )


def wave_kernel(who_ref, near_ref, next_ref, far_ref, other_ref, moves_ref, lists_ref, forward_ref, phase_ref,
                real_ref, imag_ref, top_ref, block_ref, lane_ref, rows_ref):
    yl = who_ref[0] // 2
    core = who_ref[0] % 2
    listed, group = near_ref.shape[1], near_ref.shape[2]
    columns = listed * 128
    rows_ref[...] = jnp.zeros_like(rows_ref)
    for owner in range(8):
        away = lax.bitwise_xor(owner // 2, yl)
        cross = lax.bitwise_xor(owner % 2, core)
        sources = ((0, near_ref, 0), (1, next_ref, 0), (2, far_ref, 0), (3, far_ref, 1))
        for distance, ref, at in sources:
            @pl.when(jnp.logical_and(cross == 0, away == distance))
            def _():
                for q in range(listed):
                    rows_ref[q * 128 + owner * group : q * 128 + (owner + 1) * group, 0:L] = ref[at, q]
            @pl.when(jnp.logical_and(cross == 1, away == distance))
            def _():
                for q in range(listed):
                    rows_ref[q * 128 + owner * group : q * 128 + (owner + 1) * group, 0:L] = other_ref[distance, q]
    half = forward_ref.shape[0] // 2
    eye = iota((128, 128), 0) == iota((128, 128), 1)
    for q in range(listed):
        cols = slice(q * 128, (q + 1) * 128)
        spectrum = dot_rows(forward_ref[...], rows_ref[cols, :])
        move = moves_ref[q : q + 1, :]
        chosen = (iota((SMAX, 128), 0) == move).astype(jnp.bfloat16)
        angles = dot(phase_ref[...], chosen)
        cosine = angles[:half] + angles[half : 2 * half]
        sine = angles[2 * half : 3 * half] + angles[3 * half :]
        real, imag = spectrum[:half], spectrum[half:]
        sign = 1.0 - 2.0 * (move % 2).astype(jnp.float32)
        zero = iota((half, 128), 0) == 0
        real_ref[:, cols] = jnp.where(zero, real, real * cosine + imag * sine)
        imag_ref[:, cols] = jnp.where(zero, 0.0, real * sine - imag * cosine)
        top_ref[:, cols] = jnp.broadcast_to(imag[0:1] * sign, (8, 128))
        station = to_column(lists_ref[q : q + 1, :].astype(jnp.float32), eye).astype(jnp.int32)
        block_ref[cols, :] = (iota((128, 128), 1) == station // 32).astype(jnp.bfloat16)
        lane = iota((128, 128), 1)
        lane_ref[cols, :] = jnp.logical_or(lane == station % 32, lane == 64).astype(jnp.bfloat16)


def pick_kernel(got_ref, block_ref, lane_ref, scaled_ref, level_ref, factor_ref):
    blocks = got_ref.shape[0]
    slots = blocks * CAP
    codes = got_ref[:, 2 * CAP : 2 * CAP + 8, :].astype(jnp.float32)[:, 0, :]
    start = iota((blocks, 128), 0).astype(jnp.float32) * CAP
    codes = jnp.where(iota((blocks, 128), 1) == 64, start, codes).astype(jnp.bfloat16)
    codes = jnp.concatenate([codes, jnp.zeros((128 - blocks, 128), jnp.bfloat16)], axis=0)
    low = got_ref[:, 0:CAP, :].reshape(slots, 128)
    high = got_ref[:, CAP : 2 * CAP, :].reshape(slots, 128)
    waves = jnp.concatenate([low, high], axis=1)
    width = waves.shape[1]
    eye = iota((128, 128), 0) == iota((128, 128), 1)
    total = jnp.zeros((1, 128), jnp.float32)
    listed = block_ref.shape[0] // 128
    for q in range(listed):
        cols = slice(q * 128, (q + 1) * 128)
        target = jnp.sum(
            dot(block_ref[cols, :], codes) * lane_ref[cols, :].astype(jnp.float32), axis=1, keepdims=True
        )
        chosen = jnp.where(iota((128, slots), 1).astype(jnp.float32) == target, 1.0, 0.0).astype(jnp.bfloat16)
        rows = dot(chosen, waves)
        power = jnp.sum(rows * rows, axis=1, keepdims=True) * (1.0 / width)
        present = jnp.where(target < MISSING * 0.5, 1.0, 0.0)
        safe = jnp.minimum(power, LIMIT) + epsilon
        scaled_ref[cols, :] = (rows * lax.rsqrt(safe)).astype(jnp.bfloat16)
        level_ref[q : q + 1, :] = to_row(jnp.sqrt(safe), eye)
        factor_ref[q : q + 1, :] = to_row(present * lax.rsqrt(power + epsilon), eye)
        total = total + to_row(present, eye)
    factor_ref[listed : listed + 8, :] = jnp.broadcast_to(1.0 / jnp.maximum(total, 1.0), (8, 128))


def own_kernel(scaled_ref, factor_ref, real_ref, imag_ref, top_ref, forward_ref, inverse_ref, mixed_ref, out_ref):
    half = real_ref.shape[0]
    listed = real_ref.shape[1] // 128
    sums = [jnp.zeros((half, 128), jnp.float32), jnp.zeros((half, 128), jnp.float32)]
    zero = iota((half, 128), 0) == 0
    for q in range(listed):
        cols = slice(q * 128, (q + 1) * 128)
        spectrum = dot_rows(forward_ref[...], scaled_ref[cols, :])
        real, imag = spectrum[:half], spectrum[half:]
        wave_real, wave_imag = real_ref[:, cols], imag_ref[:, cols]
        mixed_real = wave_real * real - wave_imag * imag
        straight = jnp.where(zero, top_ref[0:1, cols], wave_real)
        mixed_imag = straight * imag + wave_imag * real
        mixed_ref[:half, cols] = mixed_real.astype(jnp.bfloat16)
        mixed_ref[half:, cols] = mixed_imag.astype(jnp.bfloat16)
        weight = jnp.where(factor_ref[q : q + 1, :] > 0.0, 1.0, 0.0)
        sums[0] = sums[0] + weight * mixed_real
        sums[1] = sums[1] + weight * mixed_imag
    joined = jnp.concatenate(sums, axis=0).astype(jnp.bfloat16)
    span = 2 * half
    series = dot(inverse_ref[...], joined) * (factor_ref[listed : listed + 1, :] * (1.0 / span))
    out_ref[...] = jnp.transpose(series)


def after_kernel(mixed_ref, level_ref, factor_ref, inverse_ref, out_ref):
    span = mixed_ref.shape[0]
    listed = mixed_ref.shape[1] // 128
    weights = level_ref[...] * factor_ref[0:listed, :]
    total = jnp.zeros((span, 128), jnp.float32)
    for q in range(listed):
        total = total + weights[q : q + 1, :] * mixed_ref[:, q * 128 : (q + 1) * 128].astype(jnp.float32)
    series = dot(inverse_ref[...], total.astype(jnp.bfloat16)) * (factor_ref[listed : listed + 1, :] * (1.0 / span))
    out_ref[...] = jnp.transpose(series).astype(jnp.bfloat16)


def params():
    return pltpu.CompilerParams(vmem_limit_bytes=48 * 1024 * 1024)


def pack(status, waves):
    count, windows, width = waves.shape
    part = windows // 2
    rows = 2 * CAP + 8
    return pl.pallas_call(
        pack_kernel,
        out_shape=jax.ShapeDtypeStruct((windows, rows, 128), jnp.bfloat16),
        grid=(windows // part,),
        in_specs=[
            pl.BlockSpec((count, windows), lambda i: (0, 0)),
            pl.BlockSpec((count, part, width), lambda i: (0, i, 0)),
        ],
        out_specs=pl.BlockSpec((part, rows, 128), lambda i: (i, 0, 0)),
        compiler_params=params(),
        name="pack",
    )(status, waves)


def vmem(n):
    return [pl.BlockSpec(memory_space=pltpu.VMEM)] * n


def wave(who, near, after, far, other, moves, lists, forward, phases):
    half = forward.shape[0] // 2
    columns = lists.shape[0] * 128
    return pl.pallas_call(
        wave_kernel,
        out_shape=(
            jax.ShapeDtypeStruct((half, columns), jnp.float32),
            jax.ShapeDtypeStruct((half, columns), jnp.float32),
            jax.ShapeDtypeStruct((8, columns), jnp.float32),
            jax.ShapeDtypeStruct((columns, 128), jnp.bfloat16),
            jax.ShapeDtypeStruct((columns, 128), jnp.bfloat16),
        ),
        in_specs=[pl.BlockSpec(memory_space=pltpu.SMEM)] + vmem(8),
        out_specs=tuple(vmem(5)),
        scratch_shapes=[pltpu.VMEM((columns, forward.shape[1]), jnp.bfloat16)],
        compiler_params=params(),
        name="wave",
    )(who, near, after, far, other, moves, lists, forward, phases)


def pick(got, block, lane):
    columns = block.shape[0]
    listed = columns // 128
    return pl.pallas_call(
        pick_kernel,
        out_shape=(
            jax.ShapeDtypeStruct((columns, 256), jnp.bfloat16),
            jax.ShapeDtypeStruct((listed, 128), jnp.float32),
            jax.ShapeDtypeStruct((listed + 8, 128), jnp.float32),
        ),
        in_specs=vmem(3),
        out_specs=tuple(vmem(3)),
        compiler_params=params(),
        name="pick",
    )(got, block, lane)


def own_part(scaled, factor, real, imag, top, forward, inverse):
    span, columns = forward.shape[0], real.shape[1]
    return pl.pallas_call(
        own_kernel,
        out_shape=(
            jax.ShapeDtypeStruct((span, columns), jnp.bfloat16),
            jax.ShapeDtypeStruct((128, inverse.shape[0]), jnp.float32),
        ),
        in_specs=vmem(7),
        out_specs=tuple(vmem(2)),
        compiler_params=params(),
        name="own_part",
    )(scaled, factor, real, imag, top, forward, inverse)


def after_part(mixed, level, factor, inverse):
    return pl.pallas_call(
        after_kernel,
        out_shape=jax.ShapeDtypeStruct((128, inverse.shape[0]), jnp.bfloat16),
        in_specs=vmem(4),
        out_specs=vmem(1)[0],
        compiler_params=params(),
        name="after_part",
    )(mixed, level, factor, inverse)


def exchange(value, bit):
    return lax.ppermute(value, "tmpl", [(i, i ^ bit) for i in range(8)])


def shifted(value, by):
    axis = ("tm", "tmpl")
    count = lax.axis_size(axis)
    return lax.ppermute(value, axis, [(i, i + by) for i in range(count) if 0 <= i + by < count])


def shards(raw, avail, templates, stations, shifts):
    width = raw.shape[3]
    span = width + L + SMAX
    forward = forward_rows(span, width)
    inverse, inverse_after = inverse_rows(span, width)
    phases = phase_tables(span, SMAX)
    near = jnp.transpose(templates, (1, 0, 2))[None]
    after = exchange(near, 2)
    pair = jnp.concatenate([near, after])
    payload = pack(jnp.transpose(avail[:, 0, :]), raw[:, :, 0, :])
    got = lax.all_to_all(payload, "tm", split_axis=0, concat_axis=0, tiled=True)
    far = exchange(pair, 4)
    other = exchange(jnp.concatenate([pair, far]), 1)
    who = lax.axis_index("tmpl").reshape(1)
    real, imag, top, block, lane = wave(
        who, near, after, far, other, jnp.transpose(shifts), jnp.transpose(stations), forward, phases
    )
    scaled, level, factor = pick(got, block, lane)
    before = shifted(factor, 1)
    mixed, own = own_part(scaled, factor, real, imag, top, forward, inverse)
    late = shifted(after_part(mixed, level, before, inverse_after), -1)
    return own + late.astype(jnp.float32)


def solution(mesh):
    return jax.shard_map(
        shards,
        mesh=mesh,
        in_specs=(
            P("tm", None, "tmpl", None),
            P(None, "tmpl", "tm"),
            P("tmpl", None, None),
            P(),
            P(),
        ),
        out_specs=P(None, ("tm", "tmpl")),
        check_vma=False,
    )
```

```python
import functools
import math

import jax
import jax.numpy as jnp
import numpy as np
from jax import lax
from jax.experimental import pallas as pl
from jax.experimental.pallas import tpu as pltpu
from jax.sharding import PartitionSpec as P

L = 192
SMAX = 64
CAP = 24
GROUP = 16
MISSING = 4096.0
LIMIT = 3e38

epsilon = 1e-05


def cosine_rows(span, width):
    half = span // 2
    frequency = np.arange(half)[:, None]
    sample = np.arange(width)[None, :]
    angle = (frequency * sample % span) * (2.0 * math.pi / span)
    real = np.cos(angle)
    imag = -np.sin(angle)
    imag[0] = np.cos(math.pi * np.arange(width))
    return real, imag


def forward_rows(span, width):
    real, imag = cosine_rows(span, width)
    return jnp.asarray(np.concatenate([real, imag]).astype(jnp.bfloat16))


def inverse_rows(span, width):
    real, imag = cosine_rows(span, width)
    real, imag = 2.0 * real, 2.0 * imag
    real[0] *= 0.5
    imag[0] *= 0.5
    table = np.concatenate([real, imag])
    flip = np.where(np.arange(span // 2) % 2 == 0, 1.0, -1.0)
    after = table * np.concatenate([flip, flip])[:, None]
    return (
        jnp.asarray(table.T.astype(jnp.bfloat16)),
        jnp.asarray(after.T.astype(jnp.bfloat16)),
    )


def phase_tables(span, moves):
    angle = (np.arange(span // 2)[:, None] * np.arange(moves)[None, :] % span) * (2.0 * math.pi / span)
    parts = []
    for value in (np.cos(angle), np.sin(angle)):
        high = value.astype(jnp.bfloat16)
        parts.append(high)
        parts.append((value - high.astype(np.float64)).astype(jnp.bfloat16))
    return jnp.asarray(np.concatenate(parts))


def dot(a, b):
    return jnp.dot(a, b, preferred_element_type=jnp.float32)


def dot_rows(a, b):
    return lax.dot_general(a, b, (((1,), (1,)), ((), ())), preferred_element_type=jnp.float32)


def iota(shape, dim):
    return lax.broadcasted_iota(jnp.int32, shape, dim)


def to_row(column, eye):
    return jnp.sum(jnp.where(eye, column, 0.0), axis=0, keepdims=True)


def to_column(row, eye):
    return jnp.sum(jnp.where(eye, row, 0.0), axis=1, keepdims=True)


def pack_kernel(avail_ref, raw_ref, out_ref, waves_ref, done_ref, get_sem, put_sem):
    count, windows, width = raw_ref.shape
    parts = windows // GROUP

    def fetch(part):
        rows = pl.ds(part * GROUP, GROUP)
        return pltpu.make_async_copy(raw_ref.at[:, rows, :], waves_ref.at[part], get_sem.at[part])

    def store(part):
        rows = pl.ds(part * GROUP, GROUP)
        return pltpu.make_async_copy(done_ref.at[rows], out_ref.at[rows], put_sem.at[part])

    for part in range(parts):
        fetch(part).start()
    flags = jnp.transpose(avail_ref[...].astype(jnp.float32)).astype(jnp.bfloat16)
    place = (iota((count, 128), 0) == iota((count, 128), 1)).astype(jnp.bfloat16)
    before = (iota((count, 128), 0) < iota((count, 128), 1)).astype(jnp.bfloat16)
    code = jnp.where(dot(flags, place) > 0.5, dot(flags, before), MISSING)
    lanes = count * GROUP
    spread = (iota((128, lanes), 0) == iota((128, lanes), 1) // GROUP).astype(jnp.bfloat16)
    slot = iota((GROUP, CAP, lanes), 1).astype(jnp.float32)
    for part in range(parts):
        own = code[part * GROUP : (part + 1) * GROUP]
        wide = dot(own.astype(jnp.bfloat16), spread)
        wide = jnp.where(iota((GROUP, lanes), 1) % GROUP == iota((GROUP, lanes), 0), wide, -1.0)
        mover = jnp.where(wide[:, None, :] == slot, 1.0, 0.0).reshape(GROUP * CAP, lanes).astype(jnp.bfloat16)
        fetch(part).wait()
        moved = dot(mover, waves_ref[part].reshape(lanes, width))
        for window in range(GROUP):
            rows = moved[window * CAP : (window + 1) * CAP]
            extra = jnp.broadcast_to(own[window : window + 1], (8, 128))
            done_ref[part * GROUP + window] = jnp.concatenate([rows[:, :128], rows[:, 128:], extra], axis=0).astype(
                jnp.bfloat16
            )
        store(part).start()
    for part in range(parts):
        store(part).wait()


def table_kernel(moves_ref, lists_ref, phase_ref, cosine_ref, sine_ref, sign_ref, block_ref, lane_ref):
    half = cosine_ref.shape[0]
    eye = iota((128, 128), 0) == iota((128, 128), 1)
    for q in range(moves_ref.shape[0]):
        cols = slice(q * 128, (q + 1) * 128)
        move = moves_ref[q : q + 1, :]
        angles = dot(phase_ref[...], (iota((SMAX, 128), 0) == move).astype(jnp.bfloat16))
        cosine_ref[:, cols] = angles[:half] + angles[half : 2 * half]
        sine_ref[:, cols] = angles[2 * half : 3 * half] + angles[3 * half :]
        sign_ref[q : q + 1, :] = 1.0 - 2.0 * (move % 2).astype(jnp.float32)
        station = to_column(lists_ref[q : q + 1, :].astype(jnp.float32), eye).astype(jnp.int32)
        lane = iota((128, 128), 1)
        block_ref[cols, :] = (lane == station // 32).astype(jnp.bfloat16)
        lane_ref[cols, :] = jnp.logical_or(lane == station % 32, lane == 64).astype(jnp.bfloat16)


def pick_kernel(got_ref, block_ref, lane_ref, scaled_ref, level_ref, factor_ref):
    blocks = got_ref.shape[0]
    slots = blocks * CAP
    codes = got_ref[:, 2 * CAP : 2 * CAP + 8, :].astype(jnp.float32)[:, 0, :]
    start = iota((blocks, 128), 0).astype(jnp.float32) * CAP
    codes = jnp.where(iota((blocks, 128), 1) == 64, start, codes).astype(jnp.bfloat16)
    codes = jnp.concatenate([codes, jnp.zeros((128 - blocks, 128), jnp.bfloat16)], axis=0)
    low = got_ref[:, 0:CAP, :].reshape(slots, 128)
    high = got_ref[:, CAP : 2 * CAP, :].reshape(slots, 128)
    waves = jnp.concatenate([low, high], axis=1)
    width = waves.shape[1]
    eye = iota((128, 128), 0) == iota((128, 128), 1)
    total = jnp.zeros((1, 128), jnp.float32)
    listed = block_ref.shape[0] // 128
    for q in range(listed):
        cols = slice(q * 128, (q + 1) * 128)
        target = jnp.sum(
            dot(block_ref[cols, :], codes) * lane_ref[cols, :].astype(jnp.float32), axis=1, keepdims=True
        )
        chosen = jnp.where(iota((128, slots), 1).astype(jnp.float32) == target, 1.0, 0.0).astype(jnp.bfloat16)
        rows = dot(chosen, waves)
        power = jnp.sum(rows * rows, axis=1, keepdims=True) * (1.0 / width)
        present = jnp.where(target < MISSING * 0.5, 1.0, 0.0)
        safe = jnp.minimum(power, LIMIT) + epsilon
        scaled_ref[cols, :] = (rows * lax.rsqrt(safe)).astype(jnp.bfloat16)
        level_ref[q : q + 1, :] = to_row(jnp.sqrt(safe), eye)
        factor_ref[q : q + 1, :] = to_row(present * lax.rsqrt(power + epsilon), eye)
        total = total + to_row(present, eye)
    factor_ref[listed : listed + 8, :] = jnp.broadcast_to(1.0 / jnp.maximum(total, 1.0), (8, 128))


def own_kernel(who_ref, pair_ref, right_ref, cross_ref, left_ref, scaled_ref, factor_ref, cosine_ref, sine_ref,
               sign_ref, forward_ref, inverse_ref, mixed_ref, out_ref, rows_ref):
    half = cosine_ref.shape[0]
    listed = cosine_ref.shape[1] // 128
    span = 2 * half
    chip, core = who_ref[0] // 2, who_ref[0] % 2
    group = pair_ref.shape[2]
    rows_ref[:, 128:] = jnp.zeros((listed * 128, rows_ref.shape[1] - 128), jnp.bfloat16)
    for away, ref in enumerate((pair_ref, right_ref, cross_ref, left_ref)):
        for other in range(2):
            owner = lax.rem(chip + away, 4) * 2 + lax.rem(core + other, 2)
            for q in range(listed):
                at = pl.ds(pl.multiple_of(q * 128 + owner * group, group), group)
                rows_ref[at, 0:128] = ref[other, q]
                tail = ref[other, listed + q % 4]
                rows_ref[at, 128:L] = tail[:, : L - 128] if q < 4 else tail[:, L - 128 :]
    sums = [jnp.zeros((half, 128), jnp.float32), jnp.zeros((half, 128), jnp.float32)]
    zero = iota((half, 128), 0) == 0
    for q in range(listed):
        cols = slice(q * 128, (q + 1) * 128)
        template = dot_rows(forward_ref[...], rows_ref[cols, :])
        spectrum = dot_rows(forward_ref[...], scaled_ref[cols, :])
        real, imag = spectrum[:half], spectrum[half:]
        cosine, sine = cosine_ref[:, cols], sine_ref[:, cols]
        wave_real = template[:half] * cosine + template[half:] * sine
        wave_imag = template[:half] * sine - template[half:] * cosine
        wave_real = jnp.where(zero, template[:half], wave_real)
        wave_imag = jnp.where(zero, 0.0, wave_imag)
        straight = jnp.where(zero, template[half:] * sign_ref[q : q + 1, :], wave_real)
        mixed_real = wave_real * real - wave_imag * imag
        mixed_imag = straight * imag + wave_imag * real
        mixed_ref[:half, cols] = mixed_real.astype(jnp.bfloat16)
        mixed_ref[half:, cols] = mixed_imag.astype(jnp.bfloat16)
        weight = jnp.where(factor_ref[q : q + 1, :] > 0.0, 1.0, 0.0)
        sums[0] = sums[0] + weight * mixed_real
        sums[1] = sums[1] + weight * mixed_imag
    joined = jnp.concatenate(sums, axis=0).astype(jnp.bfloat16)
    series = dot(inverse_ref[...], joined) * (factor_ref[listed : listed + 1, :] * (1.0 / span))
    out_ref[...] = jnp.transpose(series)


def after_kernel(mixed_ref, level_ref, factor_ref, inverse_ref, out_ref):
    span = mixed_ref.shape[0]
    listed = mixed_ref.shape[1] // 128
    weights = level_ref[...] * factor_ref[0:listed, :]
    total = jnp.zeros((span, 128), jnp.float32)
    for q in range(listed):
        total = total + weights[q : q + 1, :] * mixed_ref[:, q * 128 : (q + 1) * 128].astype(jnp.float32)
    series = dot(inverse_ref[...], total.astype(jnp.bfloat16)) * (factor_ref[listed : listed + 1, :] * (1.0 / span))
    out_ref[...] = jnp.transpose(series).astype(jnp.bfloat16)


def params():
    return pltpu.CompilerParams(vmem_limit_bytes=16 * 1024 * 1024)


def vmem(n):
    return [pl.BlockSpec(memory_space=pltpu.VMEM)] * n


def pack(status, waves):
    count, windows, width = waves.shape
    parts = windows // GROUP
    shape = (windows, 2 * CAP + 8, 128)
    return pl.pallas_call(
        pack_kernel,
        out_shape=jax.ShapeDtypeStruct(shape, jnp.bfloat16),
        in_specs=vmem(1) + [pl.BlockSpec(memory_space=pl.ANY)],
        out_specs=pl.BlockSpec(memory_space=pl.ANY),
        scratch_shapes=[
            pltpu.VMEM((parts, count, GROUP, width), jnp.bfloat16),
            pltpu.VMEM(shape, jnp.bfloat16),
            pltpu.SemaphoreType.DMA((parts,)),
            pltpu.SemaphoreType.DMA((parts,)),
        ],
        compiler_params=params(),
        name="pack",
    )(status, waves)


def tables(moves, lists, phases):
    half = phases.shape[0] // 4
    listed = lists.shape[0]
    columns = listed * 128
    return pl.pallas_call(
        table_kernel,
        out_shape=(
            jax.ShapeDtypeStruct((half, columns), jnp.float32),
            jax.ShapeDtypeStruct((half, columns), jnp.float32),
            jax.ShapeDtypeStruct((listed, 128), jnp.float32),
            jax.ShapeDtypeStruct((columns, 128), jnp.bfloat16),
            jax.ShapeDtypeStruct((columns, 128), jnp.bfloat16),
        ),
        in_specs=vmem(3),
        out_specs=tuple(vmem(5)),
        compiler_params=params(),
        name="tables",
    )(moves, lists, phases)


def pick(got, block, lane):
    columns = block.shape[0]
    listed = columns // 128
    return pl.pallas_call(
        pick_kernel,
        out_shape=(
            jax.ShapeDtypeStruct((columns, 256), jnp.bfloat16),
            jax.ShapeDtypeStruct((listed, 128), jnp.float32),
            jax.ShapeDtypeStruct((listed + 8, 128), jnp.float32),
        ),
        in_specs=vmem(3),
        out_specs=tuple(vmem(3)),
        compiler_params=params(),
        name="pick",
    )(got, block, lane)


def own_part(who, blocks, scaled, factor, cosine, sine, sign, forward, inverse):
    span, columns = forward.shape[0], cosine.shape[1]
    return pl.pallas_call(
        own_kernel,
        out_shape=(
            jax.ShapeDtypeStruct((span, columns), jnp.bfloat16),
            jax.ShapeDtypeStruct((128, inverse.shape[0]), jnp.float32),
        ),
        in_specs=[pl.BlockSpec(memory_space=pltpu.SMEM)] + vmem(11),
        out_specs=tuple(vmem(2)),
        scratch_shapes=[pltpu.VMEM((columns, forward.shape[1]), jnp.bfloat16)],
        compiler_params=params(),
        name="own_part",
    )(who, *blocks, scaled, factor, cosine, sine, sign, forward, inverse)


def after_part(mixed, level, factor, inverse):
    return pl.pallas_call(
        after_kernel,
        out_shape=jax.ShapeDtypeStruct((128, inverse.shape[0]), jnp.bfloat16),
        in_specs=vmem(4),
        out_specs=vmem(1)[0],
        compiler_params=params(),
        name="after_part",
    )(mixed, level, factor, inverse)


def other_core(value):
    return lax.ppermute(value, "tmpl", [(i, i ^ 1) for i in range(8)])


def along_ring(value, by):
    pairs = []
    for i in range(lax.axis_size(("tm", "tmpl"))):
        tm, chip, core = i // 8, i // 2 % 4, i % 2
        to = (tm % 2 * 4 + chip + by) % 8
        pairs.append((i, (tm // 2 * 2 + to // 4) * 8 + to % 4 * 2 + core))
    return lax.ppermute(value, ("tm", "tmpl"), pairs)


def shifted(value, by):
    axis = ("tm", "tmpl")
    count = lax.axis_size(axis)
    return lax.ppermute(value, axis, [(i, i + by) for i in range(count) if 0 <= i + by < count])


def shards(raw, avail, templates, stations, shifts):
    width = raw.shape[3]
    span = width + L + SMAX
    forward = forward_rows(span, width)
    inverse, inverse_after = inverse_rows(span, width)
    phases = phase_tables(span, SMAX)
    own = jnp.transpose(templates, (1, 0, 2))
    tail = jnp.concatenate([own[:4, :, 128:], own[4:, :, 128:]], axis=2)
    own = jnp.concatenate([own[:, :, :128], tail], axis=0)
    other = other_core(own)
    payload = pack(jnp.transpose(avail[:, 0, :]), raw[:, :, 0, :])
    payload, other = lax.optimization_barrier((payload, other))
    got = lax.all_to_all(payload, "tm", split_axis=0, concat_axis=0, tiled=True)
    pair = jnp.stack([own, other])
    blocks = (pair, along_ring(pair, -1), along_ring(pair, 2), along_ring(pair, 1))
    who = lax.axis_index("tmpl").reshape(1)
    cosine, sine, sign, block, lane = tables(jnp.transpose(shifts), jnp.transpose(stations), phases)
    scaled, level, factor = pick(got, block, lane)
    before = shifted(factor, 1)
    mixed, stack = own_part(who, blocks, scaled, factor, cosine, sine, sign, forward, inverse)
    late = shifted(after_part(mixed, level, before, inverse_after), -1)
    return stack + late.astype(jnp.float32)


def solution(mesh):
    return jax.shard_map(
        shards,
        mesh=mesh,
        in_specs=(
            P("tm", None, "tmpl", None),
            P(None, "tmpl", "tm"),
            P("tmpl", None, None),
            P(),
            P(),
        ),
        out_specs=P(None, ("tm", "tmpl")),
        check_vma=False,
    )
```

```python
import functools
import math

import jax
import jax.numpy as jnp
import numpy as np
from jax import lax
from jax.experimental import pallas as pl
from jax.experimental.pallas import tpu as pltpu
from jax.sharding import PartitionSpec as P

L = 192
SMAX = 64
CAP = 24
GROUP = 16
MISSING = 4096.0
LIMIT = 3e38

epsilon = 1e-05


def cosine_rows(span, width):
    half = span // 2
    frequency = np.arange(half)[:, None]
    sample = np.arange(width)[None, :]
    angle = (frequency * sample % span) * (2.0 * math.pi / span)
    real = np.cos(angle)
    imag = -np.sin(angle)
    imag[0] = np.cos(math.pi * np.arange(width))
    return real, imag


def forward_rows(span, width):
    real, imag = cosine_rows(span, width)
    return jnp.asarray(np.concatenate([real, imag]).astype(jnp.bfloat16))


def inverse_rows(span, width):
    real, imag = cosine_rows(span, width)
    real, imag = 2.0 * real, 2.0 * imag
    real[0] *= 0.5
    imag[0] *= 0.5
    table = np.concatenate([real, imag])
    flip = np.where(np.arange(span // 2) % 2 == 0, 1.0, -1.0)
    after = table * np.concatenate([flip, flip])[:, None]
    return (
        jnp.asarray(table.T.astype(jnp.bfloat16)),
        jnp.asarray(after.T.astype(jnp.bfloat16)),
    )


def phase_tables(span, moves):
    angle = (np.arange(span // 2)[:, None] * np.arange(moves)[None, :] % span) * (2.0 * math.pi / span)
    parts = []
    for value in (np.cos(angle), np.sin(angle)):
        high = value.astype(jnp.bfloat16)
        parts.append(high)
        parts.append((value - high.astype(np.float64)).astype(jnp.bfloat16))
    return jnp.asarray(np.concatenate(parts))


def dot(a, b):
    return jnp.dot(a, b, preferred_element_type=jnp.float32)


def dot_rows(a, b):
    return lax.dot_general(a, b, (((1,), (1,)), ((), ())), preferred_element_type=jnp.float32)


def iota(shape, dim):
    return lax.broadcasted_iota(jnp.int32, shape, dim)


def to_row(column, eye):
    return jnp.sum(jnp.where(eye, column, 0.0), axis=0, keepdims=True)


def to_column(row, eye):
    return jnp.sum(jnp.where(eye, row, 0.0), axis=1, keepdims=True)


def pack_kernel(avail_ref, raw_ref, out_ref, waves_ref, done_ref, get_sem, put_sem):
    count, windows, width = raw_ref.shape
    parts = windows // GROUP

    def fetch(part):
        rows = pl.ds(part * GROUP, GROUP)
        return pltpu.make_async_copy(raw_ref.at[:, rows, :], waves_ref.at[part], get_sem.at[part])

    def store(part):
        rows = pl.ds(windows - (part + 1) * GROUP, GROUP)
        return pltpu.make_async_copy(done_ref.at[rows], out_ref.at[rows], put_sem.at[part])

    for part in range(parts):
        fetch(part).start()
    flags = jnp.transpose(avail_ref[...].astype(jnp.float32)).astype(jnp.bfloat16)
    place = (iota((count, 128), 0) == iota((count, 128), 1)).astype(jnp.bfloat16)
    before = (iota((count, 128), 0) < iota((count, 128), 1)).astype(jnp.bfloat16)
    code = jnp.where(dot(flags, place) > 0.5, dot(flags, before), MISSING)
    lanes = count * GROUP
    spread = (iota((128, lanes), 0) == iota((128, lanes), 1) // GROUP).astype(jnp.bfloat16)
    slot = iota((GROUP, CAP, lanes), 1).astype(jnp.float32)
    for part in range(parts):
        own = code[part * GROUP : (part + 1) * GROUP]
        wide = dot(own.astype(jnp.bfloat16), spread)
        wide = jnp.where(iota((GROUP, lanes), 1) % GROUP == iota((GROUP, lanes), 0), wide, -1.0)
        mover = jnp.where(wide[:, None, :] == slot, 1.0, 0.0).reshape(GROUP * CAP, lanes).astype(jnp.bfloat16)
        fetch(part).wait()
        moved = dot(mover, waves_ref[part].reshape(lanes, width))
        for window in range(GROUP):
            rows = moved[window * CAP : (window + 1) * CAP]
            extra = jnp.broadcast_to(own[window : window + 1], (8, 128))
            done_ref[windows - 1 - part * GROUP - window] = jnp.concatenate([rows[:, :128], rows[:, 128:], extra], axis=0).astype(
                jnp.bfloat16
            )
        store(part).start()
    for part in range(parts):
        store(part).wait()


def wave_kernel(who_ref, pair_ref, right_ref, cross_ref, left_ref, moves_ref, forward_ref, phase_ref,
                wave_ref, top_ref, rows_ref):
    listed, span = wave_ref.shape[0], wave_ref.shape[1]
    half = span // 2
    chip, core = who_ref[0] // 2, who_ref[0] % 2
    group = pair_ref.shape[2]
    rows_ref[:, 128:] = jnp.zeros((listed * 128, rows_ref.shape[1] - 128), jnp.bfloat16)
    for away, ref in enumerate((pair_ref, right_ref, cross_ref, left_ref)):
        for other in range(2):
            owner = lax.rem(chip + away, 4) * 2 + lax.rem(core + other, 2)
            for q in range(listed):
                at = pl.ds(pl.multiple_of(q * 128 + owner * group, group), group)
                rows_ref[at, 0:128] = ref[other, q]
                tail = ref[other, listed + q % 4]
                rows_ref[at, 128:L] = tail[:, : L - 128] if q < 4 else tail[:, L - 128 :]
    zero = iota((half, 128), 0) == 0
    for q in range(listed):
        move = moves_ref[q : q + 1, :]
        angles = dot(phase_ref[...], (iota((SMAX, 128), 0) == move).astype(jnp.bfloat16))
        cosine = angles[:half] + angles[half : 2 * half]
        sine = angles[2 * half : 3 * half] + angles[3 * half :]
        sign = 1.0 - 2.0 * (move % 2).astype(jnp.float32)
        if q % 2 == 0:
            spectra = dot_rows(forward_ref[...], rows_ref[q * 128 : (q + 2) * 128, :])
        spectrum = spectra[:, q % 2 * 128 : (q % 2 + 1) * 128]
        real, imag = spectrum[:half], spectrum[half:]
        wave_ref[q, :half] = jnp.where(zero, real, real * cosine + imag * sine).astype(jnp.bfloat16)
        wave_ref[q, half:] = jnp.where(zero, 0.0, real * sine - imag * cosine).astype(jnp.bfloat16)
        top_ref[q : q + 1, :] = imag[0:1] * sign


def pick_kernel(got_ref, lists_ref, scaled_ref, level_ref, factor_ref):
    blocks = got_ref.shape[0]
    slots = blocks * CAP
    codes = got_ref[:, 2 * CAP : 2 * CAP + 8, :].astype(jnp.float32)[:, 0, :]
    start = iota((blocks, 128), 0).astype(jnp.float32) * CAP
    codes = jnp.where(iota((blocks, 128), 1) == 64, start, codes).astype(jnp.bfloat16)
    codes = jnp.concatenate([codes, jnp.zeros((128 - blocks, 128), jnp.bfloat16)], axis=0)
    low = got_ref[:, 0:CAP, :].reshape(slots, 128)
    high = got_ref[:, CAP : 2 * CAP, :].reshape(slots, 128)
    waves = jnp.concatenate([low, high], axis=1)
    width = waves.shape[1]
    eye = iota((128, 128), 0) == iota((128, 128), 1)
    lane = iota((256, 128), 1)
    total = jnp.zeros((1, 128), jnp.float32)
    listed = lists_ref.shape[0]
    for pair in range(listed // 2):
        both = (2 * pair, 2 * pair + 1)
        columns = [to_column(lists_ref[q : q + 1, :].astype(jnp.float32), eye) for q in both]
        station = jnp.concatenate(columns, axis=0).astype(jnp.int32)
        holder = (lane == blocks - 1 - station // 32).astype(jnp.bfloat16)
        mask = jnp.logical_or(lane == station % 32, lane == 64)
        target = jnp.sum(jnp.where(mask, dot(holder, codes), 0.0), axis=1, keepdims=True)
        chosen = jnp.where(iota((256, slots), 1).astype(jnp.float32) == target, 1.0, 0.0).astype(jnp.bfloat16)
        rows = dot(chosen, waves)
        power = jnp.sum(rows * rows, axis=1, keepdims=True) * (1.0 / width)
        present = jnp.where(target < MISSING * 0.5, 1.0, 0.0)
        safe = jnp.minimum(power, LIMIT) + epsilon
        scaled_ref[pair * 256 : (pair + 1) * 256, :] = (rows * lax.rsqrt(safe)).astype(jnp.bfloat16)
        level = jnp.sqrt(safe)
        factor = present * lax.rsqrt(power + epsilon)
        for side, q in enumerate(both):
            at = slice(side * 128, (side + 1) * 128)
            level_ref[q : q + 1, :] = to_row(level[at], eye)
            factor_ref[q : q + 1, :] = to_row(factor[at], eye)
            total = total + to_row(present[at], eye)
    factor_ref[listed : listed + 8, :] = jnp.broadcast_to(1.0 / jnp.maximum(total, 1.0), (8, 128))


def own_kernel(wave_ref, scaled_ref, factor_ref, top_ref, forward_ref, inverse_ref, mixed_ref, out_ref):
    listed, span = wave_ref.shape[0], wave_ref.shape[1]
    half = span // 2

    sums = [jnp.zeros((half, 128), jnp.float32), jnp.zeros((half, 128), jnp.float32)]
    zero = iota((half, 128), 0) == 0
    for q in range(listed):
        if q % 2 == 0:
            spectra = dot_rows(forward_ref[...], scaled_ref[q * 128 : (q + 2) * 128, :])
        spectrum = spectra[:, q % 2 * 128 : (q % 2 + 1) * 128]
        cols = slice(q * 128, (q + 1) * 128)
        real, imag = spectrum[:half], spectrum[half:]
        wave_real = wave_ref[q, :half].astype(jnp.float32)
        wave_imag = wave_ref[q, half:].astype(jnp.float32)
        straight = jnp.where(zero, top_ref[q : q + 1, :], wave_real)
        mixed_real = wave_real * real - wave_imag * imag
        mixed_imag = straight * imag + wave_imag * real
        mixed_ref[:half, cols] = mixed_real.astype(jnp.bfloat16)
        mixed_ref[half:, cols] = mixed_imag.astype(jnp.bfloat16)
        weight = jnp.where(factor_ref[q : q + 1, :] > 0.0, 1.0, 0.0)
        sums[0] = sums[0] + weight * mixed_real
        sums[1] = sums[1] + weight * mixed_imag
    joined = jnp.concatenate(sums, axis=0).astype(jnp.bfloat16)
    series = dot(inverse_ref[...], joined) * (factor_ref[listed : listed + 1, :] * (1.0 / span))
    out_ref[...] = jnp.transpose(series)


def after_kernel(mixed_ref, level_ref, factor_ref, inverse_ref, out_ref):
    span = mixed_ref.shape[0]
    listed = mixed_ref.shape[1] // 128
    weights = level_ref[...] * factor_ref[0:listed, :]
    total = jnp.zeros((span, 128), jnp.float32)
    for q in range(listed):
        total = total + weights[q : q + 1, :] * mixed_ref[:, q * 128 : (q + 1) * 128].astype(jnp.float32)
    series = dot(inverse_ref[...], total.astype(jnp.bfloat16)) * (factor_ref[listed : listed + 1, :] * (1.0 / span))
    out_ref[...] = jnp.transpose(series).astype(jnp.bfloat16)


def params(mebibytes=16):
    return pltpu.CompilerParams(vmem_limit_bytes=mebibytes * 1024 * 1024)


def vmem(n):
    return [pl.BlockSpec(memory_space=pltpu.VMEM)] * n


def pack(status, waves):
    count, windows, width = waves.shape
    parts = windows // GROUP
    shape = (windows, 2 * CAP + 8, 128)
    return pl.pallas_call(
        pack_kernel,
        out_shape=jax.ShapeDtypeStruct(shape, jnp.bfloat16),
        in_specs=vmem(1) + [pl.BlockSpec(memory_space=pltpu.HBM)],
        out_specs=pl.BlockSpec(memory_space=pltpu.HBM),
        scratch_shapes=[
            pltpu.VMEM((parts, count, GROUP, width), jnp.bfloat16),
            pltpu.VMEM(shape, jnp.bfloat16),
            pltpu.SemaphoreType.DMA((parts,)),
            pltpu.SemaphoreType.DMA((parts,)),
        ],
        compiler_params=params(63),
        name="pack",
    )(status, waves)


def wave(who, blocks, moves, forward, phases):
    span = forward.shape[0]
    listed = moves.shape[0]
    return pl.pallas_call(
        wave_kernel,
        out_shape=(
            jax.ShapeDtypeStruct((listed, span, 128), jnp.bfloat16),
            jax.ShapeDtypeStruct((listed, 128), jnp.float32),
        ),
        in_specs=[pl.BlockSpec(memory_space=pltpu.SMEM)] + vmem(7),
        out_specs=tuple(vmem(2)),
        scratch_shapes=[pltpu.VMEM((listed * 128, forward.shape[1]), jnp.bfloat16)],
        compiler_params=params(),
        name="wave",
    )(who, *blocks, moves, forward, phases)


def pick(got, lists):
    listed = lists.shape[0]
    return pl.pallas_call(
        pick_kernel,
        out_shape=(
            jax.ShapeDtypeStruct((listed * 128, 256), jnp.bfloat16),
            jax.ShapeDtypeStruct((listed, 128), jnp.float32),
            jax.ShapeDtypeStruct((listed + 8, 128), jnp.float32),
        ),
        in_specs=vmem(2),
        out_specs=tuple(vmem(3)),
        compiler_params=params(),
        name="pick",
    )(got, lists)


def own_part(waves, scaled, factor, top, forward, inverse):
    listed, span = waves.shape[0], waves.shape[1]
    return pl.pallas_call(
        own_kernel,
        out_shape=(
            jax.ShapeDtypeStruct((span, listed * 128), jnp.bfloat16),
            jax.ShapeDtypeStruct((128, inverse.shape[0]), jnp.float32),
        ),
        in_specs=vmem(6),
        out_specs=tuple(vmem(2)),
        compiler_params=params(),
        name="own_part",
    )(waves, scaled, factor, top, forward, inverse)


def after_part(mixed, level, factor, inverse):
    return pl.pallas_call(
        after_kernel,
        out_shape=jax.ShapeDtypeStruct((128, inverse.shape[0]), jnp.bfloat16),
        in_specs=vmem(4),
        out_specs=vmem(1)[0],
        compiler_params=params(),
        name="after_part",
    )(mixed, level, factor, inverse)


def other_core(value):
    return lax.ppermute(value, "tmpl", [(i, i ^ 1) for i in range(8)])


def along_ring(value, by):
    pairs = []
    for i in range(lax.axis_size(("tm", "tmpl"))):
        tm, chip, core = i // 8, i // 2 % 4, i % 2
        to = (tm % 2 * 4 + chip + by) % 8
        pairs.append((i, (tm // 2 * 2 + to // 4) * 8 + to % 4 * 2 + core))
    return lax.ppermute(value, ("tm", "tmpl"), pairs)


def shifted(value, by):
    axis = ("tm", "tmpl")
    count = lax.axis_size(axis)
    return lax.ppermute(value, axis, [(i, i + by) for i in range(count) if 0 <= i + by < count])


def scatter_windows(value):
    count, width = lax.axis_size("tm"), lax.axis_size("tmpl")
    groups = [[(count - 1 - p) * width + j for p in range(count)] for j in range(width)]
    return lax.all_to_all(value, ("tm", "tmpl"), split_axis=0, concat_axis=0, axis_index_groups=groups, tiled=True)


def shards(raw, avail, templates, stations, shifts):
    width = raw.shape[3]
    span = width + L + SMAX
    forward = forward_rows(span, width)
    inverse, inverse_after = inverse_rows(span, width)
    phases = phase_tables(span, SMAX)
    lists = jnp.transpose(stations)
    got = scatter_windows(pack(jnp.transpose(avail[:, 0, :]), raw[:, :, 0, :]))
    own = jnp.transpose(templates, (1, 0, 2))
    tail = jnp.concatenate([own[:4, :, 128:], own[4:, :, 128:]], axis=2)
    own = jnp.concatenate([own[:, :, :128], tail], axis=0)
    pair = jnp.stack([own, other_core(own)])
    blocks = (pair, along_ring(pair, -1), along_ring(pair, 2), along_ring(pair, 1))
    who = lax.axis_index("tmpl").reshape(1)
    waves, top = wave(who, blocks, jnp.transpose(shifts), forward, phases)
    scaled, level, factor = pick(got, lists)
    before = shifted(factor, 1)
    mixed, stack = own_part(waves, scaled, factor, top, forward, inverse)
    late = shifted(after_part(mixed, level, before, inverse_after), -1)
    return stack + late.astype(jnp.float32)


def solution(mesh):
    return jax.shard_map(
        shards,
        mesh=mesh,
        in_specs=(
            P("tm", None, "tmpl", None),
            P(None, "tmpl", "tm"),
            P("tmpl", None, None),
            P(),
            P(),
        ),
        out_specs=P(None, ("tm", "tmpl")),
        check_vma=False,
    )
```

```python
import functools
import math

import jax
import jax.numpy as jnp
import numpy as np
from jax import lax
from jax.experimental import pallas as pl
from jax.experimental.pallas import tpu as pltpu
from jax.sharding import PartitionSpec as P

L = 192
SMAX = 64
CAP = 24
ROWS = 2 * CAP + 2
GROUP = 16
MISSING = 4096.0
LIMIT = 3e38

epsilon = 1e-05


def cosine_rows(span, width):
    half = span // 2
    frequency = np.arange(half)[:, None]
    sample = np.arange(width)[None, :]
    angle = (frequency * sample % span) * (2.0 * math.pi / span)
    real = np.cos(angle)
    imag = -np.sin(angle)
    imag[0] = np.cos(math.pi * np.arange(width))
    return real, imag


def forward_rows(span, width):
    real, imag = cosine_rows(span, width)
    return jnp.asarray(np.concatenate([real, imag]).astype(jnp.bfloat16))


def inverse_rows(span, width):
    real, imag = cosine_rows(span, width)
    real, imag = 2.0 * real, 2.0 * imag
    real[0] *= 0.5
    imag[0] *= 0.5
    table = np.concatenate([real, imag])
    flip = np.where(np.arange(span // 2) % 2 == 0, 1.0, -1.0)
    after = table * np.concatenate([flip, flip])[:, None]
    return (
        jnp.asarray(table.T.astype(jnp.bfloat16)),
        jnp.asarray(after.T.astype(jnp.bfloat16)),
    )


def phase_tables(span, moves):
    angle = (np.arange(span // 2)[:, None] * np.arange(moves)[None, :] % span) * (2.0 * math.pi / span)
    parts = []
    for value in (np.cos(angle), np.sin(angle)):
        high = value.astype(jnp.bfloat16)
        parts.append(high)
        parts.append((value - high.astype(np.float64)).astype(jnp.bfloat16))
    return jnp.asarray(np.concatenate(parts))


def dot(a, b):
    return jnp.dot(a, b, preferred_element_type=jnp.float32)


def dot_rows(a, b):
    return lax.dot_general(a, b, (((1,), (1,)), ((), ())), preferred_element_type=jnp.float32)


def iota(shape, dim):
    return lax.broadcasted_iota(jnp.int32, shape, dim)


def to_row(column, eye):
    return jnp.sum(jnp.where(eye, column, 0.0), axis=0, keepdims=True)


def to_column(row, eye):
    return jnp.sum(jnp.where(eye, row, 0.0), axis=1, keepdims=True)


def pack_kernel(avail_ref, raw_ref, out_ref, flags_ref, waves_ref, mover_ref, done_ref, flag_sem, get_sem, put_sem):
    count, windows, width = raw_ref.shape
    parts = windows // GROUP

    def fetch(part):
        rows = pl.ds(part * GROUP, GROUP)
        return pltpu.make_async_copy(raw_ref.at[:, rows, :], waves_ref.at[part], get_sem.at[part])

    def store(part):
        rows = pl.ds((windows - (part + 1) * GROUP) * ROWS, GROUP * ROWS)
        return pltpu.make_async_copy(done_ref.at[rows], out_ref.at[rows], put_sem.at[part])

    status = pltpu.make_async_copy(avail_ref, flags_ref, flag_sem)
    status.start()
    for part in range(parts):
        fetch(part).start()
    place = (iota((count, 128), 0) == iota((count, 128), 1)).astype(jnp.bfloat16)
    before = (iota((count, 128), 0) < iota((count, 128), 1)).astype(jnp.bfloat16)
    lanes = count * GROUP
    spread = (iota((128, lanes), 0) == iota((128, lanes), 1) // GROUP).astype(jnp.bfloat16)
    slot = iota((GROUP, CAP, lanes), 1).astype(jnp.float32)
    status.wait()
    flags = jnp.transpose(flags_ref[...].astype(jnp.float32)).astype(jnp.bfloat16)
    code = jnp.where(dot(flags, place) > 0.5, dot(flags, before), MISSING)
    wide = dot(code.astype(jnp.bfloat16), spread)
    wide = jnp.where(iota((windows, lanes), 1) % GROUP == iota((windows, lanes), 0) % GROUP, wide, -1.0)
    for part in range(parts):
        own = wide[part * GROUP : (part + 1) * GROUP]
        mover = jnp.where(own[:, None, :] == slot, 1.0, 0.0)
        mover_ref[part] = mover.reshape(GROUP * CAP, lanes).astype(jnp.bfloat16)
    for part in range(parts):
        fetch(part).wait()
        moved = dot(mover_ref[part], waves_ref[part].reshape(lanes, width))
        for index in range(GROUP):
            window = part * GROUP + index
            rows = moved[index * CAP : (index + 1) * CAP]
            note = jnp.broadcast_to(code[window : window + 1], (ROWS - 2 * CAP, 128))
            at = (windows - 1 - window) * ROWS
            block = jnp.concatenate([rows[:, :128], rows[:, 128:], note], axis=0)
            done_ref[at : at + ROWS, :] = block.astype(jnp.bfloat16)
        store(part).start()
    for part in range(parts):
        store(part).wait()


def wave_kernel(who_ref, pair_ref, right_ref, cross_ref, left_ref, lists_ref, forward_ref, phase_ref,
                wave_ref, top_ref, rows_ref):
    listed, span = wave_ref.shape[0], wave_ref.shape[1]
    half = span // 2
    chip, core = who_ref[0] // 2, who_ref[0] % 2
    group = pair_ref.shape[2]
    rows_ref[:, 128:] = jnp.zeros((listed * 128, rows_ref.shape[1] - 128), jnp.bfloat16)
    for away, ref in enumerate((pair_ref, right_ref, cross_ref, left_ref)):
        for other in range(2):
            owner = lax.rem(chip + away, 4) * 2 + lax.rem(core + other, 2)
            for q in range(listed):
                at = pl.ds(pl.multiple_of(q * 128 + owner * group, group), group)
                rows_ref[at, 0:128] = ref[other, q]
                tail = ref[other, listed + q % 4]
                rows_ref[at, 128:L] = tail[:, : L - 128] if q < 4 else tail[:, L - 128 :]
    zero = iota((half, 128), 0) == 0
    for q in range(listed):
        move = lists_ref[listed + q : listed + q + 1, :]
        angles = dot(phase_ref[...], (iota((SMAX, 128), 0) == move).astype(jnp.bfloat16))
        cosine = angles[:half] + angles[half : 2 * half]
        sine = angles[2 * half : 3 * half] + angles[3 * half :]
        sign = 1.0 - 2.0 * (move % 2).astype(jnp.float32)
        if q % 2 == 0:
            spectra = dot_rows(forward_ref[...], rows_ref[q * 128 : (q + 2) * 128, :])
        spectrum = spectra[:, q % 2 * 128 : (q % 2 + 1) * 128]
        real, imag = spectrum[:half], spectrum[half:]
        wave_ref[q, :half] = jnp.where(zero, real, real * cosine + imag * sine).astype(jnp.bfloat16)
        wave_ref[q, half:] = jnp.where(zero, 0.0, real * sine - imag * cosine).astype(jnp.bfloat16)
        top_ref[q : q + 1, :] = imag[0:1] * sign


def pick_kernel(got_ref, lists_ref, scaled_ref, level_ref, factor_ref):
    blocks = got_ref.shape[0] // ROWS
    slots = blocks * CAP
    listed = level_ref.shape[0]

    def gather(first, size):
        rows = [got_ref[block * ROWS + first : block * ROWS + first + size, :] for block in range(blocks)]
        return [value.astype(jnp.float32) for value in rows]

    low = jnp.concatenate(gather(0, CAP), axis=0).astype(jnp.bfloat16)
    high = jnp.concatenate(gather(CAP, CAP), axis=0).astype(jnp.bfloat16)
    waves = jnp.concatenate([low, high], axis=1)
    width = waves.shape[1]
    codes = jnp.concatenate([value[0:1] for value in gather(2 * CAP, 2)], axis=0)
    start = iota((blocks, 128), 0).astype(jnp.float32) * CAP
    codes = jnp.where(iota((blocks, 128), 1) == 64, start, codes).astype(jnp.bfloat16)
    codes = jnp.concatenate([codes, jnp.zeros((128 - blocks, 128), jnp.bfloat16)], axis=0)
    eye = iota((128, 128), 0) == iota((128, 128), 1)
    columns = [to_column(lists_ref[q : q + 1, :].astype(jnp.float32), eye) for q in range(listed)]
    station = jnp.concatenate(columns, axis=0).astype(jnp.int32)
    lane = iota((listed * 128, 128), 1)
    holder = (lane == blocks - 1 - station // 32).astype(jnp.bfloat16)
    mask = jnp.logical_or(lane == station % 32, lane == 64)
    targets = jnp.sum(jnp.where(mask, dot(holder, codes), 0.0), axis=1, keepdims=True)
    total = jnp.zeros((1, 128), jnp.float32)
    for pair in range(listed // 2):
        cols = slice(pair * 256, (pair + 1) * 256)
        target = targets[cols]
        chosen = jnp.where(iota((256, slots), 1).astype(jnp.float32) == target, 1.0, 0.0).astype(jnp.bfloat16)
        rows = dot(chosen, waves)
        power = jnp.sum(rows * rows, axis=1, keepdims=True) * (1.0 / width)
        present = jnp.where(target < MISSING * 0.5, 1.0, 0.0)
        safe = jnp.minimum(power, LIMIT) + epsilon
        scaled_ref[cols, :] = (rows * lax.rsqrt(safe)).astype(jnp.bfloat16)
        level = jnp.sqrt(safe)
        factor = present * lax.rsqrt(power + epsilon)
        for side in range(2):
            q = 2 * pair + side
            at = slice(side * 128, (side + 1) * 128)
            level_ref[q : q + 1, :] = to_row(level[at], eye)
            factor_ref[q : q + 1, :] = to_row(factor[at], eye)
            total = total + to_row(present[at], eye)
    factor_ref[listed : listed + 8, :] = jnp.broadcast_to(1.0 / jnp.maximum(total, 1.0), (8, 128))


def mix_kernel(wave_ref, scaled_ref, top_ref, forward_ref, mixed_ref):
    listed, span = wave_ref.shape[0], wave_ref.shape[1]
    half = span // 2
    zero = iota((half, 128), 0) == 0
    for q in range(listed):
        if q % 2 == 0:
            spectra = dot_rows(forward_ref[...], scaled_ref[q * 128 : (q + 2) * 128, :])
        spectrum = spectra[:, q % 2 * 128 : (q % 2 + 1) * 128]
        cols = slice(q * 128, (q + 1) * 128)
        real, imag = spectrum[:half], spectrum[half:]
        wave_real = wave_ref[q, :half].astype(jnp.float32)
        wave_imag = wave_ref[q, half:].astype(jnp.float32)
        straight = jnp.where(zero, top_ref[q : q + 1, :], wave_real)
        mixed_ref[:half, cols] = (wave_real * real - wave_imag * imag).astype(jnp.bfloat16)
        mixed_ref[half:, cols] = (straight * imag + wave_imag * real).astype(jnp.bfloat16)


def weighted_stack(mixed_ref, weights, scale, inverse_ref):
    span = mixed_ref.shape[0]
    total = jnp.zeros((span, 128), jnp.float32)
    for q in range(mixed_ref.shape[1] // 128):
        total = total + weights[q : q + 1, :] * mixed_ref[:, q * 128 : (q + 1) * 128].astype(jnp.float32)
    series = dot(inverse_ref[...], total.astype(jnp.bfloat16)) * (scale * (1.0 / span))
    return jnp.transpose(series)


def late_kernel(mixed_ref, level_ref, factor_ref, inverse_ref, out_ref):
    listed = level_ref.shape[0]
    weights = level_ref[...] * factor_ref[0:listed, :]
    out_ref[...] = weighted_stack(mixed_ref, weights, factor_ref[listed : listed + 1, :], inverse_ref).astype(jnp.bfloat16)


def own_kernel(mixed_ref, factor_ref, inverse_ref, late_ref, out_ref):
    listed = mixed_ref.shape[1] // 128
    weights = jnp.where(factor_ref[0:listed, :] > 0.0, 1.0, 0.0)
    out_ref[...] = weighted_stack(mixed_ref, weights, factor_ref[listed : listed + 1, :], inverse_ref)


def params(mebibytes=16):
    return pltpu.CompilerParams(vmem_limit_bytes=mebibytes * 1024 * 1024)


def vmem(n):
    return [pl.BlockSpec(memory_space=pltpu.VMEM)] * n


def pack(status, waves):
    count, windows, width = waves.shape
    parts = windows // GROUP
    shape = (windows * ROWS, 128)
    return pl.pallas_call(
        pack_kernel,
        out_shape=jax.ShapeDtypeStruct(shape, jnp.bfloat16),
        in_specs=[pl.BlockSpec(memory_space=pltpu.HBM)] * 2,
        out_specs=pl.BlockSpec(memory_space=pltpu.HBM),
        scratch_shapes=[
            pltpu.VMEM(status.shape, jnp.int32),
            pltpu.VMEM((parts, count, GROUP, width), jnp.bfloat16),
            pltpu.VMEM((parts, GROUP * CAP, count * GROUP), jnp.bfloat16),
            pltpu.VMEM(shape, jnp.bfloat16),
            pltpu.SemaphoreType.DMA,
            pltpu.SemaphoreType.DMA((parts,)),
            pltpu.SemaphoreType.DMA((parts,)),
        ],
        compiler_params=params(63),
        name="pack",
    )(status, waves)


def wave(who, blocks, lists, forward, phases):
    span = forward.shape[0]
    listed = lists.shape[0] // 2
    return pl.pallas_call(
        wave_kernel,
        out_shape=(
            jax.ShapeDtypeStruct((listed, span, 128), jnp.bfloat16),
            jax.ShapeDtypeStruct((listed, 128), jnp.float32),
        ),
        in_specs=[pl.BlockSpec(memory_space=pltpu.SMEM)] + vmem(7),
        out_specs=tuple(vmem(2)),
        scratch_shapes=[pltpu.VMEM((listed * 128, forward.shape[1]), jnp.bfloat16)],
        compiler_params=params(),
        name="wave",
    )(who, *blocks, lists, forward, phases)


def pick(got, lists):
    listed = lists.shape[0] // 2
    return pl.pallas_call(
        pick_kernel,
        out_shape=(
            jax.ShapeDtypeStruct((listed * 128, 256), jnp.bfloat16),
            jax.ShapeDtypeStruct((listed, 128), jnp.float32),
            jax.ShapeDtypeStruct((listed + 8, 128), jnp.float32),
        ),
        in_specs=vmem(2),
        out_specs=tuple(vmem(3)),
        compiler_params=params(),
        name="pick",
    )(got, lists)


def mix(waves, scaled, top, forward):
    listed, span = waves.shape[0], waves.shape[1]
    return pl.pallas_call(
        mix_kernel,
        out_shape=jax.ShapeDtypeStruct((span, listed * 128), jnp.bfloat16),
        in_specs=vmem(4),
        out_specs=vmem(1)[0],
        compiler_params=params(),
        name="mix",
    )(waves, scaled, top, forward)


def late_part(mixed, level, factor, inverse):
    return pl.pallas_call(
        late_kernel,
        out_shape=jax.ShapeDtypeStruct((128, inverse.shape[0]), jnp.bfloat16),
        in_specs=vmem(4),
        out_specs=vmem(1)[0],
        compiler_params=params(),
        name="late_part",
    )(mixed, level, factor, inverse)


def own_part(mixed, factor, inverse, late):
    return pl.pallas_call(
        own_kernel,
        out_shape=jax.ShapeDtypeStruct((128, inverse.shape[0]), jnp.float32),
        in_specs=vmem(3) + [pl.BlockSpec(memory_space=pl.ANY)],
        out_specs=vmem(1)[0],
        compiler_params=params(),
        name="own_part",
    )(mixed, factor, inverse, late)


def other_core(value):
    return lax.ppermute(value, "tmpl", [(i, i ^ 1) for i in range(8)])


def along_ring(value, by):
    pairs = []
    for i in range(lax.axis_size(("tm", "tmpl"))):
        tm, chip, core = i // 8, i // 2 % 4, i % 2
        to = (tm % 2 * 4 + chip + by) % 8
        pairs.append((i, (tm // 2 * 2 + to // 4) * 8 + to % 4 * 2 + core))
    return lax.ppermute(value, ("tm", "tmpl"), pairs)


def shifted(value, by):
    axis = ("tm", "tmpl")
    count = lax.axis_size(axis)
    return lax.ppermute(value, axis, [(i, i + by) for i in range(count) if 0 <= i + by < count])


def scatter_windows(value):
    count, width = lax.axis_size("tm"), lax.axis_size("tmpl")
    groups = [[(count - 1 - p) * width + j for p in range(count)] for j in range(width)]
    pairs = value.reshape(count, ROWS // 2, 2, 128)
    got = lax.all_to_all(pairs, ("tm", "tmpl"), split_axis=0, concat_axis=0, axis_index_groups=groups, tiled=True)
    return got.reshape(value.shape)


def shards(raw, avail, templates, stations, shifts):
    width = raw.shape[3]
    span = width + L + SMAX
    forward = forward_rows(span, width)
    inverse, inverse_after = inverse_rows(span, width)
    phases = phase_tables(span, SMAX)
    lists = jnp.concatenate([jnp.transpose(stations), jnp.transpose(shifts)], axis=0)
    got = scatter_windows(pack(jnp.transpose(avail[:, 0, :]), raw[:, :, 0, :]))
    own = jnp.transpose(templates, (1, 0, 2))
    tail = jnp.concatenate([own[:4, :, 128:], own[4:, :, 128:]], axis=2)
    own = jnp.concatenate([own[:, :, :128], tail], axis=0)
    pair = jnp.stack([own, other_core(own)])
    blocks = (pair, along_ring(pair, -1), along_ring(pair, 2), along_ring(pair, 1))
    who = lax.axis_index("tmpl").reshape(1)
    waves, top = wave(who, blocks, lists, forward, phases)
    scaled, level, factor = pick(got, lists)
    before = shifted(factor, 1)
    mixed = mix(waves, scaled, top, forward)
    late = late_part(mixed, level, before, inverse_after)
    stack = own_part(mixed, factor, inverse, late)
    return stack + shifted(late, -1).astype(jnp.float32)


def solution(mesh):
    return jax.shard_map(
        shards,
        mesh=mesh,
        in_specs=(
            P("tm", None, "tmpl", None),
            P(None, "tmpl", "tm"),
            P("tmpl", None, None),
            P(),
            P(),
        ),
        out_specs=P(None, ("tm", "tmpl")),
        check_vma=False,
    )
```

```python
import functools
import math

import jax
import jax.numpy as jnp
import numpy as np
from jax import lax
from jax.experimental import pallas as pl
from jax.experimental.pallas import tpu as pltpu
from jax.sharding import PartitionSpec as P

L = 192
SMAX = 64
CAP = 24
ROWS = 2 * CAP + 2
GROUP = 16
FIRST = 64
MISSING = 4096.0
LIMIT = 3e38

epsilon = 1e-05


def cosine_rows(span, width):
    half = span // 2
    frequency = np.arange(half)[:, None]
    sample = np.arange(width)[None, :]
    angle = (frequency * sample % span) * (2.0 * math.pi / span)
    real = np.cos(angle)
    imag = -np.sin(angle)
    imag[0] = np.cos(math.pi * np.arange(width))
    return real, imag


def forward_rows(span, width):
    real, imag = cosine_rows(span, width)
    return jnp.asarray(np.concatenate([real, imag]).astype(jnp.bfloat16))


def inverse_rows(span, width):
    real, imag = cosine_rows(span, width)
    real, imag = 2.0 * real, 2.0 * imag
    real[0] *= 0.5
    imag[0] *= 0.5
    table = np.concatenate([real, imag])
    flip = np.where(np.arange(span // 2) % 2 == 0, 1.0, -1.0)
    after = table * np.concatenate([flip, flip])[:, None]
    return (
        jnp.asarray(table.T.astype(jnp.bfloat16)),
        jnp.asarray(after.T.astype(jnp.bfloat16)),
    )


def phase_table(span, moves):
    angle = (np.arange(span // 2)[:, None] * np.arange(moves)[None, :] % span) * (2.0 * math.pi / span)
    return jnp.asarray(np.concatenate([np.cos(angle), np.sin(angle)]).astype(jnp.bfloat16))


def dot(a, b):
    return jnp.dot(a, b, preferred_element_type=jnp.float32)


def dot_rows(a, b):
    return lax.dot_general(a, b, (((1,), (1,)), ((), ())), preferred_element_type=jnp.float32)


def iota(shape, dim):
    return lax.broadcasted_iota(jnp.int32, shape, dim)


def to_row(column, eye):
    return jnp.sum(jnp.where(eye, column, 0.0), axis=0, keepdims=True)


def to_column(row, eye):
    return jnp.sum(jnp.where(eye, row, 0.0), axis=1, keepdims=True)


def pack_kernel(avail_ref, raw_ref, out_ref, flags_ref, waves_ref, mover_ref, done_ref, flag_sem, get_sem, put_sem):
    count, windows, width = raw_ref.shape
    parts = windows // GROUP

    def fetch(part):
        rows = pl.ds(part * GROUP, GROUP)
        return pltpu.make_async_copy(raw_ref.at[:, rows, :], waves_ref.at[part], get_sem.at[part])

    def store(part):
        rows = pl.ds((windows - (part + 1) * GROUP) * ROWS, GROUP * ROWS)
        return pltpu.make_async_copy(done_ref.at[rows], out_ref.at[rows], put_sem.at[part])

    status = pltpu.make_async_copy(avail_ref, flags_ref, flag_sem)
    status.start()
    for part in range(parts):
        fetch(part).start()
    place = (iota((count, 128), 0) == iota((count, 128), 1) - FIRST).astype(jnp.bfloat16)
    before = (iota((count, 128), 0) < iota((count, 128), 1) - FIRST).astype(jnp.bfloat16)
    lanes = count * GROUP
    spread = (iota((128, lanes), 0) - FIRST == iota((128, lanes), 1) // GROUP).astype(jnp.bfloat16)
    slot = iota((GROUP, CAP, lanes), 1).astype(jnp.float32)
    status.wait()
    flags = jnp.transpose(flags_ref[...].astype(jnp.float32)).astype(jnp.bfloat16)
    code = jnp.where(dot(flags, place) > 0.5, dot(flags, before), MISSING)
    wide = dot(code.astype(jnp.bfloat16), spread)
    wide = jnp.where(iota((windows, lanes), 1) % GROUP == iota((windows, lanes), 0) % GROUP, wide, -1.0)
    for part in range(parts):
        own = wide[part * GROUP : (part + 1) * GROUP]
        mover = jnp.where(own[:, None, :] == slot, 1.0, 0.0)
        mover_ref[part] = mover.reshape(GROUP * CAP, lanes).astype(jnp.bfloat16)
    for part in range(parts):
        fetch(part).wait()
        moved = dot(mover_ref[part], waves_ref[part].reshape(lanes, width))
        for index in range(GROUP):
            window = part * GROUP + index
            rows = moved[index * CAP : (index + 1) * CAP]
            note = jnp.broadcast_to(code[window : window + 1], (ROWS - 2 * CAP, 128))
            at = (windows - 1 - window) * ROWS
            block = jnp.concatenate([rows[:, :128], rows[:, 128:], note], axis=0)
            done_ref[at : at + ROWS, :] = block.astype(jnp.bfloat16)
        store(part).start()
    for part in range(parts):
        store(part).wait()


def find_kernel(lists_ref, find_ref):
    listed = lists_ref.shape[0] // 2
    eye = iota((128, 128), 0) == iota((128, 128), 1)
    lane = iota((128, 128), 1)
    for q in range(listed):
        station = to_column(lists_ref[q : q + 1, :].astype(jnp.float32), eye).astype(jnp.int32)
        block = lane == FIRST - 1 - station // 32
        place = jnp.logical_or(lane == FIRST + station % 32, lane == FIRST + 32)
        find_ref[q * 128 : (q + 1) * 128, :] = jnp.logical_or(block, place).astype(jnp.bfloat16)


def pick_kernel(got_ref, find_ref, scaled_ref, level_ref, factor_ref):
    blocks = got_ref.shape[0] // ROWS
    slots = blocks * CAP
    listed = level_ref.shape[0]

    def gather(first, size):
        rows = [got_ref[block * ROWS + first : block * ROWS + first + size, :] for block in range(blocks)]
        return [value.astype(jnp.float32) for value in rows]

    codes = jnp.concatenate([value[0:1] for value in gather(2 * CAP, 2)], axis=0)
    lane = iota((blocks, 128), 1)
    codes = jnp.where(jnp.logical_and(lane >= FIRST, lane < FIRST + 32), codes, 0.0)
    codes = jnp.where(lane == FIRST + 32, iota((blocks, 128), 0).astype(jnp.float32) * CAP, codes)
    codes = jnp.concatenate([codes, jnp.zeros((128 - blocks, 128), jnp.float32)], axis=0).astype(jnp.bfloat16)
    find = find_ref[...]
    targets = jnp.sum(dot(find, codes) * find.astype(jnp.float32), axis=1, keepdims=True)
    low = jnp.concatenate(gather(0, CAP), axis=0).astype(jnp.bfloat16)
    high = jnp.concatenate(gather(CAP, CAP), axis=0).astype(jnp.bfloat16)
    waves = jnp.concatenate([low, high], axis=1)
    width = waves.shape[1]
    eye = iota((128, 128), 0) == iota((128, 128), 1)
    total = jnp.zeros((1, 128), jnp.float32)
    for pair in range(listed // 2):
        cols = slice(pair * 256, (pair + 1) * 256)
        target = targets[cols]
        chosen = jnp.where(iota((256, slots), 1).astype(jnp.float32) == target, 1.0, 0.0).astype(jnp.bfloat16)
        rows = dot(chosen, waves)
        power = jnp.sum(rows * rows, axis=1, keepdims=True) * (1.0 / width)
        present = jnp.where(target < MISSING * 0.5, 1.0, 0.0)
        safe = jnp.minimum(power, LIMIT) + epsilon
        scaled_ref[cols, :] = (rows * lax.rsqrt(safe)).astype(jnp.bfloat16)
        level = jnp.sqrt(safe)
        factor = present * lax.rsqrt(power + epsilon)
        for side in range(2):
            q = 2 * pair + side
            at = slice(side * 128, (side + 1) * 128)
            level_ref[q : q + 1, :] = to_row(level[at], eye)
            factor_ref[q : q + 1, :] = to_row(factor[at], eye)
            total = total + to_row(present[at], eye)
    factor_ref[listed : listed + 8, :] = jnp.broadcast_to(1.0 / jnp.maximum(total, 1.0), (8, 128))


def mix_kernel(who_ref, pair_ref, right_ref, cross_ref, left_ref, lists_ref, scaled_ref, forward_ref, phase_ref,
               mixed_ref, rows_ref):
    listed, span = lists_ref.shape[0] // 2, mixed_ref.shape[0]
    half = span // 2
    chip, core = who_ref[0] // 2, who_ref[0] % 2
    group = pair_ref.shape[2]
    rows_ref[:, 128:] = jnp.zeros((listed * 128, rows_ref.shape[1] - 128), jnp.bfloat16)
    for away, ref in enumerate((pair_ref, right_ref, cross_ref, left_ref)):
        for other in range(2):
            owner = lax.rem(chip + away, 4) * 2 + lax.rem(core + other, 2)
            for q in range(listed):
                at = pl.ds(pl.multiple_of(q * 128 + owner * group, group), group)
                rows_ref[at, 0:128] = ref[other, q]
                tail = ref[other, listed + q % 4]
                rows_ref[at, 128:L] = tail[:, : L - 128] if q < 4 else tail[:, L - 128 :]
    zero = iota((half, 256), 0) == 0
    for pair in range(listed // 2):
        cols = slice(pair * 256, (pair + 1) * 256)
        first = listed + 2 * pair
        move = jnp.concatenate([lists_ref[first : first + 1, :], lists_ref[first + 1 : first + 2, :]], axis=1)
        angles = dot(phase_ref[...], (iota((SMAX, 256), 0) == move).astype(jnp.bfloat16))
        cosine, sine = angles[:half], angles[half:]
        sign = 1.0 - 2.0 * (move % 2).astype(jnp.float32)
        template = dot_rows(forward_ref[...], rows_ref[cols, :])
        spectrum = dot_rows(forward_ref[...], scaled_ref[cols, :])
        real, imag = spectrum[:half], spectrum[half:]
        wave_real = template[:half] * cosine + template[half:] * sine
        wave_imag = template[:half] * sine - template[half:] * cosine
        wave_real = jnp.where(zero, template[:half], wave_real)
        wave_imag = jnp.where(zero, 0.0, wave_imag)
        straight = jnp.where(zero, template[half:] * sign, wave_real)
        mixed_ref[:half, cols] = (wave_real * real - wave_imag * imag).astype(jnp.bfloat16)
        mixed_ref[half:, cols] = (straight * imag + wave_imag * real).astype(jnp.bfloat16)


def weighted_stack(mixed_ref, weights, scale, inverse_ref):
    span = mixed_ref.shape[0]
    total = jnp.zeros((span, 128), jnp.float32)
    for q in range(mixed_ref.shape[1] // 128):
        total = total + weights[q : q + 1, :] * mixed_ref[:, q * 128 : (q + 1) * 128].astype(jnp.float32)
    series = dot(inverse_ref[...], total.astype(jnp.bfloat16)) * (scale * (1.0 / span))
    return jnp.transpose(series)


def late_kernel(mixed_ref, level_ref, factor_ref, inverse_ref, out_ref):
    listed = level_ref.shape[0]
    weights = level_ref[...] * factor_ref[0:listed, :]
    out_ref[...] = weighted_stack(mixed_ref, weights, factor_ref[listed : listed + 1, :], inverse_ref).astype(jnp.bfloat16)


def own_kernel(mixed_ref, factor_ref, inverse_ref, late_ref, out_ref):
    listed = mixed_ref.shape[1] // 128
    weights = jnp.where(factor_ref[0:listed, :] > 0.0, 1.0, 0.0)
    out_ref[...] = weighted_stack(mixed_ref, weights, factor_ref[listed : listed + 1, :], inverse_ref)


def params(mebibytes=16):
    return pltpu.CompilerParams(vmem_limit_bytes=mebibytes * 1024 * 1024)


def vmem(n):
    return [pl.BlockSpec(memory_space=pltpu.VMEM)] * n


def pack(status, waves):
    count, windows, width = waves.shape
    parts = windows // GROUP
    shape = (windows * ROWS, 128)
    return pl.pallas_call(
        pack_kernel,
        out_shape=jax.ShapeDtypeStruct(shape, jnp.bfloat16),
        in_specs=[pl.BlockSpec(memory_space=pltpu.HBM)] * 2,
        out_specs=pl.BlockSpec(memory_space=pltpu.HBM),
        scratch_shapes=[
            pltpu.VMEM(status.shape, jnp.int32),
            pltpu.VMEM((parts, count, GROUP, width), jnp.bfloat16),
            pltpu.VMEM((parts, GROUP * CAP, count * GROUP), jnp.bfloat16),
            pltpu.VMEM(shape, jnp.bfloat16),
            pltpu.SemaphoreType.DMA,
            pltpu.SemaphoreType.DMA((parts,)),
            pltpu.SemaphoreType.DMA((parts,)),
        ],
        compiler_params=params(63),
        name="pack",
    )(status, waves)


def find(lists):
    columns = lists.shape[0] // 2 * 128
    return pl.pallas_call(
        find_kernel,
        out_shape=jax.ShapeDtypeStruct((columns, 128), jnp.bfloat16),
        in_specs=vmem(1),
        out_specs=vmem(1)[0],
        compiler_params=params(),
        name="find",
    )(lists)


def pick(got, found):
    columns = found.shape[0]
    listed = columns // 128
    return pl.pallas_call(
        pick_kernel,
        out_shape=(
            jax.ShapeDtypeStruct((columns, 256), jnp.bfloat16),
            jax.ShapeDtypeStruct((listed, 128), jnp.float32),
            jax.ShapeDtypeStruct((listed + 8, 128), jnp.float32),
        ),
        in_specs=vmem(2),
        out_specs=tuple(vmem(3)),
        compiler_params=params(),
        name="pick",
    )(got, found)


def mix(who, blocks, lists, scaled, forward, phases):
    columns = scaled.shape[0]
    return pl.pallas_call(
        mix_kernel,
        out_shape=jax.ShapeDtypeStruct((forward.shape[0], columns), jnp.bfloat16),
        in_specs=[pl.BlockSpec(memory_space=pltpu.SMEM)] + vmem(8),
        out_specs=vmem(1)[0],
        scratch_shapes=[pltpu.VMEM((columns, forward.shape[1]), jnp.bfloat16)],
        compiler_params=params(),
        name="mix",
    )(who, *blocks, lists, scaled, forward, phases)


def late_part(mixed, level, factor, inverse):
    return pl.pallas_call(
        late_kernel,
        out_shape=jax.ShapeDtypeStruct((128, inverse.shape[0]), jnp.bfloat16),
        in_specs=vmem(4),
        out_specs=vmem(1)[0],
        compiler_params=params(),
        name="late_part",
    )(mixed, level, factor, inverse)


def own_part(mixed, factor, inverse, late):
    return pl.pallas_call(
        own_kernel,
        out_shape=jax.ShapeDtypeStruct((128, inverse.shape[0]), jnp.float32),
        in_specs=vmem(3) + [pl.BlockSpec(memory_space=pl.ANY)],
        out_specs=vmem(1)[0],
        compiler_params=params(),
        name="own_part",
    )(mixed, factor, inverse, late)


def other_core(value):
    return lax.ppermute(value, "tmpl", [(i, i ^ 1) for i in range(8)])


def along_ring(value, by):
    pairs = []
    for i in range(lax.axis_size(("tm", "tmpl"))):
        tm, chip, core = i // 8, i // 2 % 4, i % 2
        to = (tm % 2 * 4 + chip + by) % 8
        pairs.append((i, (tm // 2 * 2 + to // 4) * 8 + to % 4 * 2 + core))
    return lax.ppermute(value, ("tm", "tmpl"), pairs)


def shifted(value, by):
    axis = ("tm", "tmpl")
    count = lax.axis_size(axis)
    return lax.ppermute(value, axis, [(i, i + by) for i in range(count) if 0 <= i + by < count])


def scatter_windows(value):
    count, width = lax.axis_size("tm"), lax.axis_size("tmpl")
    groups = [[(count - 1 - p) * width + j for p in range(count)] for j in range(width)]
    pairs = value.reshape(count, ROWS // 2, 2, 128)
    got = lax.all_to_all(pairs, ("tm", "tmpl"), split_axis=0, concat_axis=0, axis_index_groups=groups, tiled=True)
    return got.reshape(value.shape)


def shards(raw, avail, templates, stations, shifts):
    width = raw.shape[3]
    span = width + L + SMAX
    forward = forward_rows(span, width)
    inverse, inverse_after = inverse_rows(span, width)
    phases = phase_table(span, SMAX)
    lists = jnp.concatenate([jnp.transpose(stations), jnp.transpose(shifts)], axis=0)
    got = scatter_windows(pack(jnp.transpose(avail[:, 0, :]), raw[:, :, 0, :]))
    own = jnp.transpose(templates, (1, 0, 2))
    tail = jnp.concatenate([own[:4, :, 128:], own[4:, :, 128:]], axis=2)
    own = jnp.concatenate([own[:, :, :128], tail], axis=0)
    pair = jnp.stack([own, other_core(own)])
    blocks = (pair, along_ring(pair, -1), along_ring(pair, 2), along_ring(pair, 1))
    who = lax.axis_index("tmpl").reshape(1)
    scaled, level, factor = pick(got, find(lists))
    before = shifted(factor, 1)
    mixed = mix(who, blocks, lists, scaled, forward, phases)
    late = late_part(mixed, level, before, inverse_after)
    stack = own_part(mixed, factor, inverse, late)
    return stack + shifted(late, -1).astype(jnp.float32)


def solution(mesh):
    return jax.shard_map(
        shards,
        mesh=mesh,
        in_specs=(
            P("tm", None, "tmpl", None),
            P(None, "tmpl", "tm"),
            P("tmpl", None, None),
            P(),
            P(),
        ),
        out_specs=P(None, ("tm", "tmpl")),
        check_vma=False,
    )
```

```python
import functools
import math

import jax
import jax.numpy as jnp
import numpy as np
from jax import lax
from jax.experimental import pallas as pl
from jax.experimental.pallas import tpu as pltpu
from jax.sharding import PartitionSpec as P

L = 192
SMAX = 64
CAP = 24
ROWS = 2 * CAP + 2
GROUP = 16
FIRST = 64
MISSING = 4096.0
LIMIT = 3e38

epsilon = 1e-05


def cosine_rows(span, width):
    half = span // 2
    frequency = np.arange(half)[:, None]
    sample = np.arange(width)[None, :]
    angle = (frequency * sample % span) * (2.0 * math.pi / span)
    real = np.cos(angle)
    imag = -np.sin(angle)
    imag[0] = np.cos(math.pi * np.arange(width))
    return real, imag


def forward_rows(span, width):
    real, imag = cosine_rows(span, width)
    return jnp.asarray(np.concatenate([real, imag]).astype(jnp.bfloat16))


def inverse_rows(span, width):
    real, imag = cosine_rows(span, width)
    real, imag = 2.0 * real, 2.0 * imag
    real[0] *= 0.5
    imag[0] *= 0.5
    table = np.concatenate([real, imag])
    flip = np.where(np.arange(span // 2) % 2 == 0, 1.0, -1.0)
    after = table * np.concatenate([flip, flip])[:, None]
    return (
        jnp.asarray(table.T.astype(jnp.bfloat16)),
        jnp.asarray(after.T.astype(jnp.bfloat16)),
    )


def phase_table(span, moves):
    angle = (np.arange(span // 2)[:, None] * np.arange(moves)[None, :] % span) * (2.0 * math.pi / span)
    return jnp.asarray(np.concatenate([np.cos(angle), np.sin(angle)]).astype(jnp.bfloat16))


def dot(a, b):
    return jnp.dot(a, b, preferred_element_type=jnp.float32)


def dot_rows(a, b):
    return lax.dot_general(a, b, (((1,), (1,)), ((), ())), preferred_element_type=jnp.float32)


def iota(shape, dim):
    return lax.broadcasted_iota(jnp.int32, shape, dim)


def to_row(column, eye):
    return jnp.sum(jnp.where(eye, column, 0.0), axis=0, keepdims=True)


def to_column(row, eye):
    return jnp.sum(jnp.where(eye, row, 0.0), axis=1, keepdims=True)


def pack_kernel(avail_ref, raw_ref, out_ref, flags_ref, waves_ref, mover_ref, done_ref, flag_sem, get_sem, put_sem):
    count, windows, width = raw_ref.shape
    parts = windows // GROUP

    def fetch(part):
        rows = pl.ds(part * GROUP, GROUP)
        return pltpu.make_async_copy(raw_ref.at[:, rows, :], waves_ref.at[part], get_sem.at[part])

    def store(part):
        rows = pl.ds((windows - (part + 1) * GROUP) * ROWS, GROUP * ROWS)
        return pltpu.make_async_copy(done_ref.at[rows], out_ref.at[rows], put_sem.at[part])

    status = pltpu.make_async_copy(avail_ref, flags_ref, flag_sem)
    status.start()
    for part in range(parts // 2):
        fetch(part).start()
    place = (iota((count, 128), 0) == iota((count, 128), 1) - FIRST).astype(jnp.bfloat16)
    before = (iota((count, 128), 0) < iota((count, 128), 1) - FIRST).astype(jnp.bfloat16)
    lanes = count * GROUP
    spread = (iota((128, lanes), 0) - FIRST == iota((128, lanes), 1) // GROUP).astype(jnp.bfloat16)
    slot = iota((GROUP, CAP, lanes), 1).astype(jnp.float32)
    status.wait()
    flags = jnp.transpose(flags_ref[...].astype(jnp.float32)).astype(jnp.bfloat16)
    code = jnp.where(dot(flags, place) > 0.5, dot(flags, before), MISSING)
    wide = dot(code.astype(jnp.bfloat16), spread)
    wide = jnp.where(iota((windows, lanes), 1) % GROUP == iota((windows, lanes), 0) % GROUP, wide, -1.0)
    for part in range(parts):
        own = wide[part * GROUP : (part + 1) * GROUP]
        mover = jnp.where(own[:, None, :] == slot, 1.0, 0.0)
        mover_ref[part] = mover.reshape(GROUP * CAP, lanes).astype(jnp.bfloat16)
    for part in range(parts // 2, parts):
        fetch(part).start()
    for part in range(parts):
        fetch(part).wait()
        moved = dot(mover_ref[part], waves_ref[part].reshape(lanes, width))
        for index in range(GROUP):
            window = part * GROUP + index
            rows = moved[index * CAP : (index + 1) * CAP]
            note = jnp.broadcast_to(code[window : window + 1], (ROWS - 2 * CAP, 128))
            at = (windows - 1 - window) * ROWS
            block = jnp.concatenate([rows[:, :128], rows[:, 128:], note], axis=0)
            done_ref[at : at + ROWS, :] = block.astype(jnp.bfloat16)
        store(part).start()
    for part in range(parts):
        store(part).wait()


def find_kernel(lists_ref, find_ref):
    listed = lists_ref.shape[0] // 2
    eye = iota((128, 128), 0) == iota((128, 128), 1)
    lane = iota((128, 128), 1)
    for q in range(listed):
        station = to_column(lists_ref[q : q + 1, :].astype(jnp.float32), eye).astype(jnp.int32)
        block = lane == FIRST - 1 - station // 32
        place = jnp.logical_or(lane == FIRST + station % 32, lane == FIRST + 32)
        find_ref[q * 128 : (q + 1) * 128, :] = jnp.logical_or(block, place).astype(jnp.bfloat16)


def pick_kernel(got_ref, find_ref, scaled_ref, level_ref, factor_ref):
    blocks = got_ref.shape[0] // ROWS
    slots = blocks * CAP
    listed = level_ref.shape[0]

    def gather(first, size):
        rows = [got_ref[block * ROWS + first : block * ROWS + first + size, :] for block in range(blocks)]
        return [value.astype(jnp.float32) for value in rows]

    codes = jnp.concatenate([value[0:1] for value in gather(2 * CAP, 2)], axis=0)
    lane = iota((blocks, 128), 1)
    codes = jnp.where(jnp.logical_and(lane >= FIRST, lane < FIRST + 32), codes, 0.0)
    codes = jnp.where(lane == FIRST + 32, iota((blocks, 128), 0).astype(jnp.float32) * CAP, codes)
    codes = jnp.concatenate([codes, jnp.zeros((128 - blocks, 128), jnp.float32)], axis=0).astype(jnp.bfloat16)
    find = find_ref[...]
    targets = jnp.sum(dot(find, codes) * find.astype(jnp.float32), axis=1, keepdims=True)
    low = jnp.concatenate(gather(0, CAP), axis=0).astype(jnp.bfloat16)
    high = jnp.concatenate(gather(CAP, CAP), axis=0).astype(jnp.bfloat16)
    waves = jnp.concatenate([low, high], axis=1)
    width = waves.shape[1]
    eye = iota((128, 128), 0) == iota((128, 128), 1)
    total = jnp.zeros((1, 128), jnp.float32)
    for pair in range(listed // 2):
        cols = slice(pair * 256, (pair + 1) * 256)
        target = targets[cols]
        chosen = jnp.where(iota((256, slots), 1).astype(jnp.float32) == target, 1.0, 0.0).astype(jnp.bfloat16)
        rows = dot(chosen, waves)
        power = jnp.sum(rows * rows, axis=1, keepdims=True) * (1.0 / width)
        present = jnp.where(target < MISSING * 0.5, 1.0, 0.0)
        safe = jnp.minimum(power, LIMIT) + epsilon
        scaled_ref[cols, :] = (rows * lax.rsqrt(safe)).astype(jnp.bfloat16)
        level = jnp.sqrt(safe)
        factor = present * lax.rsqrt(power + epsilon)
        for side in range(2):
            q = 2 * pair + side
            at = slice(side * 128, (side + 1) * 128)
            level_ref[q : q + 1, :] = to_row(level[at], eye)
            factor_ref[q : q + 1, :] = to_row(factor[at], eye)
            total = total + to_row(present[at], eye)
    factor_ref[listed : listed + 8, :] = jnp.broadcast_to(1.0 / jnp.maximum(total, 1.0), (8, 128))


def mix_kernel(pair_ref, right_ref, cross_ref, left_ref, lists_ref, scaled_ref, forward_ref, phase_ref,
               mixed_ref, rows_ref):
    listed, span = lists_ref.shape[0] // 2, mixed_ref.shape[0]
    half = span // 2
    who = lax.axis_index("tmpl")
    chip, core = who // 2, who % 2
    group = pair_ref.shape[2]
    rows_ref[:, 128:] = jnp.zeros((listed * 128, rows_ref.shape[1] - 128), jnp.bfloat16)
    for away, ref in enumerate((pair_ref, right_ref, cross_ref, left_ref)):
        for other in range(2):
            owner = lax.rem(chip + away, 4) * 2 + lax.rem(core + other, 2)
            for q in range(listed):
                at = pl.ds(pl.multiple_of(q * 128 + owner * group, group), group)
                rows_ref[at, 0:128] = ref[other, q]
                tail = ref[other, listed + q % 4]
                rows_ref[at, 128:L] = tail[:, : L - 128] if q < 4 else tail[:, L - 128 :]
    zero = iota((half, 256), 0) == 0
    for pair in range(listed // 2):
        cols = slice(pair * 256, (pair + 1) * 256)
        first = listed + 2 * pair
        move = jnp.concatenate([lists_ref[first : first + 1, :], lists_ref[first + 1 : first + 2, :]], axis=1)
        angles = dot(phase_ref[...], (iota((SMAX, 256), 0) == move).astype(jnp.bfloat16))
        cosine, sine = angles[:half], angles[half:]
        sign = 1.0 - 2.0 * (move % 2).astype(jnp.float32)
        template = dot_rows(forward_ref[...], rows_ref[cols, :])
        spectrum = dot_rows(forward_ref[...], scaled_ref[cols, :])
        real, imag = spectrum[:half], spectrum[half:]
        wave_real = template[:half] * cosine + template[half:] * sine
        wave_imag = template[:half] * sine - template[half:] * cosine
        wave_real = jnp.where(zero, template[:half], wave_real)
        wave_imag = jnp.where(zero, 0.0, wave_imag)
        straight = jnp.where(zero, template[half:] * sign, wave_real)
        mixed_ref[:half, cols] = (wave_real * real - wave_imag * imag).astype(jnp.bfloat16)
        mixed_ref[half:, cols] = (straight * imag + wave_imag * real).astype(jnp.bfloat16)


def weighted_stack(mixed_ref, weights, scale, inverse_ref):
    span = mixed_ref.shape[0]
    total = jnp.zeros((span, 128), jnp.float32)
    for q in range(mixed_ref.shape[1] // 128):
        total = total + weights[q : q + 1, :] * mixed_ref[:, q * 128 : (q + 1) * 128].astype(jnp.float32)
    series = dot(inverse_ref[...], total.astype(jnp.bfloat16)) * (scale * (1.0 / span))
    return jnp.transpose(series)


def late_kernel(mixed_ref, level_ref, factor_ref, inverse_ref, out_ref):
    listed = level_ref.shape[0]
    weights = level_ref[...] * factor_ref[0:listed, :]
    out_ref[...] = weighted_stack(mixed_ref, weights, factor_ref[listed : listed + 1, :], inverse_ref).astype(jnp.bfloat16)


def own_kernel(mixed_ref, factor_ref, inverse_ref, late_ref, out_ref):
    listed = mixed_ref.shape[1] // 128
    weights = jnp.where(factor_ref[0:listed, :] > 0.0, 1.0, 0.0)
    out_ref[...] = weighted_stack(mixed_ref, weights, factor_ref[listed : listed + 1, :], inverse_ref)


def params(mebibytes=16):
    return pltpu.CompilerParams(vmem_limit_bytes=mebibytes * 1024 * 1024)


def vmem(n):
    return [pl.BlockSpec(memory_space=pltpu.VMEM)] * n


def pack(status, waves):
    count, windows, width = waves.shape
    parts = windows // GROUP
    shape = (windows * ROWS, 128)
    return pl.pallas_call(
        pack_kernel,
        out_shape=jax.ShapeDtypeStruct(shape, jnp.bfloat16),
        in_specs=[pl.BlockSpec(memory_space=pltpu.HBM)] * 2,
        out_specs=pl.BlockSpec(memory_space=pltpu.HBM),
        scratch_shapes=[
            pltpu.VMEM(status.shape, jnp.int32),
            pltpu.VMEM((parts, count, GROUP, width), jnp.bfloat16),
            pltpu.VMEM((parts, GROUP * CAP, count * GROUP), jnp.bfloat16),
            pltpu.VMEM(shape, jnp.bfloat16),
            pltpu.SemaphoreType.DMA,
            pltpu.SemaphoreType.DMA((parts,)),
            pltpu.SemaphoreType.DMA((parts,)),
        ],
        compiler_params=params(63),
        name="pack",
    )(status, waves)


def find(lists):
    columns = lists.shape[0] // 2 * 128
    return pl.pallas_call(
        find_kernel,
        out_shape=jax.ShapeDtypeStruct((columns, 128), jnp.bfloat16),
        in_specs=vmem(1),
        out_specs=vmem(1)[0],
        compiler_params=params(),
        name="find",
    )(lists)


def pick(got, found):
    columns = found.shape[0]
    listed = columns // 128
    return pl.pallas_call(
        pick_kernel,
        out_shape=(
            jax.ShapeDtypeStruct((columns, 256), jnp.bfloat16),
            jax.ShapeDtypeStruct((listed, 128), jnp.float32),
            jax.ShapeDtypeStruct((listed + 8, 128), jnp.float32),
        ),
        in_specs=vmem(2),
        out_specs=tuple(vmem(3)),
        compiler_params=params(),
        name="pick",
    )(got, found)


def mix(blocks, lists, scaled, forward, phases):
    columns = scaled.shape[0]
    return pl.pallas_call(
        mix_kernel,
        out_shape=jax.ShapeDtypeStruct((forward.shape[0], columns), jnp.bfloat16),
        in_specs=vmem(8),
        out_specs=vmem(1)[0],
        scratch_shapes=[pltpu.VMEM((columns, forward.shape[1]), jnp.bfloat16)],
        compiler_params=params(),
        name="mix",
    )(*blocks, lists, scaled, forward, phases)


def late_part(mixed, level, factor, inverse):
    return pl.pallas_call(
        late_kernel,
        out_shape=jax.ShapeDtypeStruct((128, inverse.shape[0]), jnp.bfloat16),
        in_specs=vmem(4),
        out_specs=vmem(1)[0],
        compiler_params=params(),
        name="late_part",
    )(mixed, level, factor, inverse)


def own_part(mixed, factor, inverse, late):
    return pl.pallas_call(
        own_kernel,
        out_shape=jax.ShapeDtypeStruct((128, inverse.shape[0]), jnp.float32),
        in_specs=vmem(3) + [pl.BlockSpec(memory_space=pl.ANY)],
        out_specs=vmem(1)[0],
        compiler_params=params(),
        name="own_part",
    )(mixed, factor, inverse, late)


def other_core(value):
    return lax.ppermute(value, "tmpl", [(i, i ^ 1) for i in range(8)])


def along_ring(value, by):
    pairs = []
    for i in range(lax.axis_size(("tm", "tmpl"))):
        tm, chip, core = i // 8, i // 2 % 4, i % 2
        to = (tm % 2 * 4 + chip + by) % 8
        pairs.append((i, (tm // 2 * 2 + to // 4) * 8 + to % 4 * 2 + core))
    return lax.ppermute(value, ("tm", "tmpl"), pairs)


def shifted(value, by):
    axis = ("tm", "tmpl")
    count = lax.axis_size(axis)
    return lax.ppermute(value, axis, [(i, i + by) for i in range(count) if 0 <= i + by < count])


def scatter_windows(value):
    count, width = lax.axis_size("tm"), lax.axis_size("tmpl")
    groups = [[(count - 1 - p) * width + j for p in range(count)] for j in range(width)]
    pairs = value.reshape(count, ROWS // 2, 2, 128)
    got = lax.all_to_all(pairs, ("tm", "tmpl"), split_axis=0, concat_axis=0, axis_index_groups=groups, tiled=True)
    return got.reshape(value.shape)


def shards(raw, avail, templates, stations, shifts):
    width = raw.shape[3]
    span = width + L + SMAX
    forward = forward_rows(span, width)
    inverse, inverse_after = inverse_rows(span, width)
    phases = phase_table(span, SMAX)
    lists = jnp.concatenate([jnp.transpose(stations), jnp.transpose(shifts)], axis=0)
    got = scatter_windows(pack(jnp.transpose(avail[:, 0, :]), raw[:, :, 0, :]))
    own = jnp.transpose(templates, (1, 0, 2))
    tail = jnp.concatenate([own[:4, :, 128:], own[4:, :, 128:]], axis=2)
    own = jnp.concatenate([own[:, :, :128], tail], axis=0)
    pair = jnp.stack([own, other_core(own)])
    blocks = (pair, along_ring(pair, -1), along_ring(pair, 2), along_ring(pair, 1))
    scaled, level, factor = pick(got, find(lists))
    before = shifted(factor, 1)
    mixed = mix(blocks, lists, scaled, forward, phases)
    late = late_part(mixed, level, before, inverse_after)
    stack = own_part(mixed, factor, inverse, late)
    return stack + shifted(late, -1).astype(jnp.float32)


def solution(mesh):
    return jax.shard_map(
        shards,
        mesh=mesh,
        in_specs=(
            P("tm", None, "tmpl", None),
            P(None, "tmpl", "tm"),
            P("tmpl", None, None),
            P(),
            P(),
        ),
        out_specs=P(None, ("tm", "tmpl")),
        check_vma=False,
    )
```
